256 devices in a mesh: seq: 2 (over core), expert: 16 (over x, y), tensor: 8 (over z).
Axes of the slice: x: 4, y: 4, z: 8, core: 2. Of those that a mesh axis runs over, the one named last changes fastest.
Arguments:
- tokens: bfloat16 [2048, 6400], P('expert', ('seq', 'tensor')), may hold values from -6 to 6
- expert_ids: int32 [2048], P('expert'), may hold values from 0 to 15, as said below
- gate_weights: float32 [2048], P('expert'), may hold values from 0.3 to 1
- gate_up_codes: float32 [16, 2, 1280, 10240], P('expert', None, None, ('seq', 'tensor')), may hold values from 0 to 1048575, as said below
- gate_up_scales: float32 [16, 2, 50, 10240], P('expert', None, None, ('seq', 'tensor')), may hold values from 0.001375 to 0.0055
- down_codes: float32 [16, 2048, 6400], P('expert', ('seq', 'tensor')), may hold values from 0 to 1048575, as said below
- down_scales: float32 [16, 80, 6400], P('expert', ('seq', 'tensor')), may hold values from 0.001087033 to 0.004348132
- shared_gate_up_codes: float32 [2, 1280, 10240], P(None, 'expert', ('seq', 'tensor')), may hold values from 0 to 1048575, as said below
- shared_gate_up_scales: float32 [2, 50, 10240], P(None, None, ('seq', 'tensor')), may hold values from 0.001375 to 0.0055
- shared_down_codes: float32 [2048, 6400], P(('seq', 'tensor'), 'expert'), may hold values from 0 to 1048575, as said below
- shared_down_scales: float32 [80, 6400], P(('seq', 'tensor')), may hold values from 0.001087033 to 0.004348132
Outputs:
- mixed: bfloat16 [2048, 6400], P('expert', ('seq', 'tensor'))
The draws below stay inside these ranges and needn't reach their ends.
Inputs may be any that keep to these rules, and one draw needn't show every extreme that they name: `expert_ids`: among the 128 tokens of each aligned block no expert is named more than 16 times; in every draw one expert is named exactly 16 times in every block. `gate_up_codes`: every entry is a whole number; its five base-16 digits are the codes. `down_codes`: every entry is a whole number; its five base-16 digits are the codes. `shared_gate_up_codes`: every entry is a whole number; its five base-16 digits are the codes. `shared_down_codes`: every entry is a whole number; its five base-16 digits are the codes.
All inputs are finite; a program needn't handle non-finite values.
Results may differ from the reference program's by a relative error of at most 0.022.
Values may be sent and summed in bfloat16 or wider, within the bound.
A program may use at most 192 MiB of HBM per device.

```python
import math
import jax
import jax.numpy as jnp
from jax import lax

D = 6400
FF = 10240
FF_SH = 10240
GROUP = 128
TOK_DEV = 128
EXPERTS = 16
TOKENS = 2048
CAP = 16
N_SEQ = 2
N_TENSOR = 8


def draw_expert_ids(key, part):
    key = jax.random.fold_in(key, 11)
    favored = jax.random.randint(jax.random.fold_in(key, 1), (), 0, EXPERTS)
    prefer = jax.random.randint(jax.random.fold_in(key, 2), (EXPERTS - 1,), 0, 4) * 32768
    others = (EXPERTS - 1) * CAP

    def one_block(block_index):
        block_key = jax.random.fold_in(key, 100 + block_index)
        score_key, order_key = jax.random.split(block_key)
        places = jnp.arange(others, dtype=jnp.int32)
        owner = places // CAP
        scores = (jax.random.randint(score_key, (others,), 0, 65536) + prefer[owner]) * 4096 + places
        order = jnp.argsort(-scores)
        chosen = owner[order[:TOK_DEV - CAP]]
        chosen = chosen + (chosen >= favored).astype(jnp.int32)
        listed = jnp.concatenate([jnp.full((CAP,), favored, jnp.int32), chosen.astype(jnp.int32)])
        return jax.random.permutation(order_key, listed)
    result = jax.vmap(one_block)(jnp.arange(TOKENS // TOK_DEV, dtype=jnp.int32))
    return result.reshape(TOKENS).astype(jnp.int32)


def draw_gate_up_codes(key, part):
    key = jax.random.fold_in(key, 21)
    return jax.random.randint(key, (EXPERTS, 2, D // 5, FF), 0, 1048576).astype(jnp.float32)


def draw_down_codes(key, part):
    key = jax.random.fold_in(key, 22)
    return jax.random.randint(key, (EXPERTS, FF // 5, D), 0, 1048576).astype(jnp.float32)


def draw_shared_gate_up_codes(key, part):
    key = jax.random.fold_in(key, 23)
    return jax.random.randint(key, (2, D // 5, FF_SH), 0, 1048576).astype(jnp.float32)


def draw_shared_down_codes(key, part):
    key = jax.random.fold_in(key, 24)
    return jax.random.randint(key, (FF_SH // 5, D), 0, 1048576).astype(jnp.float32)


def level_of(key, extent, pieces, smallest, high):
    loudness = 1.0
    for axis_at, blocks in pieces:
        heights = jax.random.uniform(jax.random.fold_in(jax.random.fold_in(key, 6), axis_at), (blocks,), jnp.float32, smallest / len(pieces), high / len(pieces))
        loudness = loudness * jnp.repeat(jnp.exp(heights), extent[axis_at] // blocks).reshape((-1,) + (1,) * (len(extent) - 1 - axis_at))
    return loudness


def centred(rng, shape, spread, reach, cuts=(), held_as=jnp.bfloat16):
    values = spread * jax.random.normal(rng, shape, jnp.float32)
    if cuts:
        values = values * level_of(rng, shape, cuts, -0.22, 0.18)
    return jnp.clip(values, -reach, reach).astype(held_as)


def setup_inputs(seed: int = 0) -> dict:
    arg_keys = jax.random.split(jax.random.key(seed), 12)
    return {
        "tokens": centred(arg_keys[0], (TOKENS, D), 1.0, 6.0, ((0, 16), (1, 16))),
        "expert_ids": draw_expert_ids(jax.random.fold_in(arg_keys[11], 71), 0),
        "gate_weights": jnp.clip(0.3 + 0.7 * jax.random.uniform(arg_keys[2], (TOKENS,), jnp.float32) ** level_of(arg_keys[2], (TOKENS,), ((0, 16),), -0.2, 0.2), 0.3, 1.0),
        "gate_up_codes": draw_gate_up_codes(jax.random.fold_in(arg_keys[11], 71), 0),
        "gate_up_scales": jnp.clip(jnp.exp(math.log(0.0055) - 1.3862944 * jax.random.uniform(arg_keys[4], (EXPERTS, 2, D // GROUP, FF), jnp.float32) ** level_of(arg_keys[4], (EXPERTS, 2, D // GROUP, FF), ((0, 16), (3, 16)), -0.2, 0.2)), 0.001375, 0.0055),
        "down_codes": draw_down_codes(jax.random.fold_in(arg_keys[11], 71), 0),
        "down_scales": jnp.clip(jnp.exp(math.log(0.004348132) - 1.3862944 * jax.random.uniform(arg_keys[6], (EXPERTS, FF // GROUP, D), jnp.float32) ** level_of(arg_keys[6], (EXPERTS, FF // GROUP, D), ((0, 16), (1, 16)), -0.2, 0.2)), 0.001087033, 0.004348132),
        "shared_gate_up_codes": draw_shared_gate_up_codes(jax.random.fold_in(arg_keys[11], 71), 0),
        "shared_gate_up_scales": jnp.clip(jnp.exp(math.log(0.0055) - 1.3862944 * jax.random.uniform(arg_keys[8], (2, D // GROUP, FF_SH), jnp.float32) ** level_of(arg_keys[8], (2, D // GROUP, FF_SH), ((2, 16),), -0.2, 0.2)), 0.001375, 0.0055),
        "shared_down_codes": draw_shared_down_codes(jax.random.fold_in(arg_keys[11], 71), 0),
        "shared_down_scales": jnp.clip(jnp.exp(math.log(0.004348132) - 1.3862944 * jax.random.uniform(arg_keys[10], (FF_SH // GROUP, D), jnp.float32) ** level_of(arg_keys[10], (FF_SH // GROUP, D), ((0, 16),), -0.2, 0.2)), 0.001087033, 0.004348132),
    }


digit_scales = [1.0, 0.0625, 0.00390625, 0.000244140625, 0.0000152587890625, 0.00000095367431640625]


def unpack(packed, scales):
    word_rows = packed.shape[0]
    columns = packed.shape[1]
    blocks = scales.shape[0] // 5
    group_size = word_rows // blocks
    words = packed.reshape(blocks, group_size, columns)
    grouped = scales.reshape(blocks, 5, 1, columns)
    lower = jnp.floor(words * digit_scales[0])
    digits = []
    for place in range(5):
        higher = jnp.floor(words * digit_scales[place + 1])
        code = lower - 16.0 * higher - 8.0
        digits.append((code * grouped[:, place]).astype(jnp.bfloat16))
        lower = higher
    return jnp.stack(digits, axis=1).reshape(word_rows * 5, columns)


def expert_ffn(inputs, gu_packed, gu_scales, dn_packed, dn_scales):
    w_gate = unpack(gu_packed[0], gu_scales[0])
    w_up = unpack(gu_packed[1], gu_scales[1])
    w_down = unpack(dn_packed, dn_scales)
    gate_act = jnp.dot(inputs, w_gate, preferred_element_type=jnp.float32)
    up_act = jnp.dot(inputs, w_up, preferred_element_type=jnp.float32)
    hidden = (jax.nn.silu(gate_act) * up_act).astype(jnp.bfloat16)
    shards = N_SEQ * N_TENSOR
    hidden_width = hidden.shape[1]
    block = hidden_width // shards
    hidden_blocks = hidden.reshape(hidden.shape[0], shards, block).transpose(1, 0, 2)
    down_blocks = w_down.reshape(shards, block, w_down.shape[1])

    def add_block(total, items):
        hidden_part, down_part = items
        term = jnp.dot(hidden_part, down_part, preferred_element_type=jnp.float32).astype(jnp.bfloat16)
        term = lax.optimization_barrier(term)
        return total + term.astype(jnp.float32), None

    result, _ = lax.scan(add_block, jnp.zeros((hidden.shape[0], w_down.shape[1]), jnp.float32),
                         (hidden_blocks, down_blocks))
    return result


def reference(tokens, expert_ids, gate_weights, gate_up_codes, gate_up_scales, down_codes, down_scales,
              shared_gate_up_codes, shared_gate_up_scales, shared_down_codes, shared_down_scales):
    blocks = TOKENS // TOK_DEV
    onehot = (expert_ids[:, None] == jnp.arange(EXPERTS, dtype=jnp.int32)[None, :]).astype(jnp.int32)
    counted = jnp.cumsum(onehot.reshape(blocks, TOK_DEV, EXPERTS), axis=1).reshape(TOKENS, EXPERTS)
    ranking = jnp.sum(counted * onehot, axis=1) - 1
    slot_index = (jnp.arange(TOKENS, dtype=jnp.int32) // TOK_DEV) * CAP + ranking
    width_slots = EXPERTS * CAP

    def one_expert(carry, items):
        gu_packed, gu_scales, dn_packed, dn_scales, expert = items
        mine = expert_ids == expert
        target = jnp.where(mine, slot_index, width_slots).astype(jnp.int32)
        buffer = jnp.zeros((width_slots, D), jnp.bfloat16).at[target].set(tokens, mode="drop")
        result = expert_ffn(buffer, gu_packed, gu_scales, dn_packed, dn_scales)
        picked = result[jnp.minimum(slot_index, width_slots - 1)]
        return carry + jnp.where(mine[:, None], picked, jnp.float32(0.0)), None

    routed, _ = lax.scan(one_expert, jnp.zeros((TOKENS, D), jnp.float32),
                         (gate_up_codes, gate_up_scales, down_codes, down_scales,
                          jnp.arange(EXPERTS, dtype=jnp.int32)))
    shared = expert_ffn(tokens, shared_gate_up_codes, shared_gate_up_scales, shared_down_codes, shared_down_scales)
    return (shared + gate_weights[:, None] * routed).astype(jnp.bfloat16)
```

```python
import functools

import jax
import jax.numpy as jnp
from jax import lax
from jax.experimental import pallas as pl
from jax.experimental.pallas import tpu as pltpu
from jax.sharding import PartitionSpec as P

MESH = pl.DeviceIdType.MESH
F32 = jnp.float32
BF16 = jnp.bfloat16
I32 = jnp.int32

D = 6400
HID = 640
SLOTS = 256
TOK = 128
BLK = 400
HALF_A = 208
NZ = 8


def al(value, multiple):
    return pl.multiple_of(value, multiple)


def kernel(
    tokens,
    ids,
    gate_w,
    gu_codes,
    gu_scales,
    dn_codes,
    dn_scales,
    sgu_codes,
    sgu_scales,
    sdn_codes,
    sdn_scales,
    out,
    rgu,
    rdn,
    gu_all,
    dn_all,
    weights,
    wdown,
    xs_t,
    xs,
    tk_t,
    tk,
    acc_g,
    acc_u,
    hidden,
    hidden_sh,
    part_r,
    part_s,
    sib_r,
    sib_s,
    psend_r,
    precv_r,
    msend_r,
    mrecv_r,
    psend_s,
    precv_s,
    msend_s,
    mrecv_s,
    select,
    disp,
    disp_in,
    back,
    back_in,
    own_r,
    own_s,
    wsend,
    wrecv,
    zsend,
    zrecv,
    asend,
    arecv,
    rsend,
    rrecv,
    lsem,
):
    core = lax.axis_index("seq")
    exp = lax.axis_index("expert")
    z = lax.axis_index("tensor")
    ex = exp // 4
    ey = lax.rem(exp, 4)
    other = 1 - core
    zplus = lax.rem(z + 1, NZ)
    zminus = lax.rem(z + NZ - 1, NZ)

    local_gu = []
    for b in range(10):
        rows = pl.ds(128 * b, 128)
        cp = pltpu.make_async_copy(gu_codes.at[:, rows, :], rgu.at[:, rows, :], lsem.at[b])
        cp.start()
        local_gu.append(cp)
    local_dn = pltpu.make_async_copy(dn_codes, rdn, lsem.at[10])
    local_own = pltpu.make_async_copy(
        sgu_codes, gu_all.at[:, pl.ds(al(80 * exp, 80), 80), :], lsem.at[11]
    )
    local_own.start()
    local_dn.start()

    barrier = pltpu.get_barrier_semaphore()

    def greet(k, _):
        pl.semaphore_signal(
            barrier, inc=1, device_id={"expert": lax.rem(exp + k, 16)}, device_id_type=MESH
        )
        return 0

    lax.fori_loop(1, 16, greet, 0)
    pl.semaphore_signal(barrier, inc=1, device_id={"seq": other}, device_id_type=MESH)
    pl.semaphore_signal(barrier, inc=1, device_id={"tensor": zplus}, device_id_type=MESH)
    pl.semaphore_signal(barrier, inc=1, device_id={"tensor": zminus}, device_id_type=MESH)
    pl.semaphore_wait(barrier, 18)

    sent = []

    def copy(src, dst, ssem, rsem, device):
        return pltpu.make_async_remote_copy(
            src_ref=src,
            dst_ref=dst,
            send_sem=ssem,
            recv_sem=rsem,
            device_id=device,
            device_id_type=MESH,
        )

    def push(src, dst, ssem, rsem, device):
        cp = copy(src, dst, ssem, rsem, device)
        cp.start()
        sent.append(cp)

    def region(piece, ee, half):
        if piece < 2:
            off, size = ((0, 80), (0, 40), (40, 40))[half]
            return gu_all.at[piece, pl.ds(al(80 * ee + off, 8), size), :]
        base = 200 * (piece - 2)
        off, size = ((0, 200), (0, 104), (104, 96))[half]
        return dn_all.at[pl.ds(al(400 * ee + (base + off), 8), size), :]

    class Piece:
        def __init__(self, piece):
            self.piece = piece
            self.by_x = piece % 2 == 0
            self.a = ex if self.by_x else ey
            self.b = ey if self.by_x else ex

        def block(self, da, db):
            a = lax.rem(self.a + da + 4, 4)
            b = lax.rem(self.b + db + 4, 4)
            return a * 4 + b if self.by_x else b * 4 + a

        def send(self, sem, da, db, half, step_a, step_b):
            ref = region(self.piece, self.block(da, db), half)
            s = 20 * self.piece + sem
            push(ref, ref, wsend.at[s], wrecv.at[s], {"expert": self.block(step_a, step_b)})

        def wait(self, sem, da, db, half):
            ref = region(self.piece, self.block(da, db), half)
            s = 20 * self.piece + sem
            copy(ref, ref, wsend.at[s], wrecv.at[s], {"expert": self.block(1, 0)}).wait_recv()

        def stage2(self, q, da):
            self.send(4 + 4 * q, da, 0, 0, 0, 1)
            self.send(5 + 4 * q, da, 0, 0, 0, -1)

        def stage2_forward(self, q, da):
            self.wait(4 + 4 * q, da, -1, 0)
            self.send(6 + 4 * q, da, -1, 1, 0, 1)
            self.wait(5 + 4 * q, da, 1, 0)
            self.send(7 + 4 * q, da, 1, 2, 0, -1)

        def stage2_end(self, q, da):
            self.wait(6 + 4 * q, da, 2, 1)
            self.wait(7 + 4 * q, da, 2, 2)

        def r0(self):
            self.send(0, 0, 0, 0, 1, 0)
            self.send(1, 0, 0, 0, -1, 0)
            self.stage2(0, 0)

        def r1(self):
            self.wait(0, -1, 0, 0)
            self.send(2, -1, 0, 1, 1, 0)
            self.stage2(1, -1)
            self.wait(1, 1, 0, 0)
            self.send(3, 1, 0, 2, -1, 0)
            self.stage2(2, 1)
            self.stage2_forward(0, 0)

        def r2(self):
            self.wait(2, 2, 0, 1)
            self.wait(3, 2, 0, 2)
            self.stage2(3, 2)
            self.stage2_forward(1, -1)
            self.stage2_forward(2, 1)
            self.stage2_end(0, 0)

        def r3(self):
            self.stage2_forward(3, 2)
            self.stage2_end(1, -1)
            self.stage2_end(2, 1)

        def r4(self):
            self.stage2_end(3, 2)

        def arrived(self, r):
            return (
                ((0, 0),),
                ((-1, 0), (1, 0), (0, -1), (0, 1)),
                ((2, 0), (-1, -1), (-1, 1), (1, -1), (1, 1), (0, 2)),
                ((2, -1), (2, 1), (-1, 2), (1, 2)),
                ((2, 2),),
            )[r]

    gate, up, down_a, down_b = (Piece(i) for i in range(4))

    class Gather:
        def __init__(self, ref, which):
            self.ref = ref
            self.base = 17 * which

        def rows(self, c, dz, part):
            off, size = ((0, BLK), (0, HALF_A), (HALF_A, BLK - HALF_A))[part]
            start = 3200 * c + BLK * lax.rem(z + dz + NZ, NZ) + off
            return self.ref.at[pl.ds(al(start, 16), size), :]

        def to_plus(self, s, dz, part):
            ref = self.rows(core, dz, part)
            push(ref, ref, zsend.at[self.base + s], zrecv.at[self.base + s], {"tensor": zplus})

        def to_minus(self, s, dz, part):
            ref = self.rows(core, dz, part)
            k = self.base + 4 + s
            push(ref, ref, zsend.at[k], zrecv.at[k], {"tensor": zminus})

        def to_sibling(self, s, dz, part):
            ref = self.rows(core, dz, part)
            k = self.base + 8 + s
            push(ref, ref, zsend.at[k], zrecv.at[k], {"seq": other})

        def wait(self, s, c, dz, part):
            ref = self.rows(c, dz, part)
            k = self.base + s
            copy(ref, ref, zsend.at[k], zrecv.at[k], {"seq": other}).wait_recv()

        def r0(self):
            self.to_plus(0, 0, 0)
            self.to_minus(0, 0, 0)
            self.to_sibling(0, 0, 0)

        def step(self, r):
            part = 0 if r < 3 else 1
            self.wait(r - 1, core, -r, 0)
            self.to_plus(r, -r, part)
            self.wait(4 + r - 1, core, r, 0)
            self.to_minus(r, r, 0 if r < 3 else 2)
            self.to_sibling(2 * r - 1, -r, 0)
            self.to_sibling(2 * r, r, 0)

        def last(self):
            self.wait(3, core, 4, 1)
            self.to_sibling(7, 4, 1)
            self.wait(7, core, 4, 2)
            self.to_sibling(8, 4, 2)
            self.wait(8, other, 0, 0)
            for r in (1, 2, 3):
                self.wait(8 + 2 * r - 1, other, -r, 0)
                self.wait(8 + 2 * r, other, r, 0)
            self.wait(15, other, 4, 1)
            self.wait(16, other, 4, 2)

    slots = Gather(xs_t, 0)
    toks = Gather(tk_t, 1)

    class Scatter:
        def __init__(self, which, part, sib, psend, precv, msend, mrecv):
            self.base = 9 * which
            self.part, self.sib = part, sib
            self.psend, self.precv, self.msend, self.mrecv = psend, precv, msend, mrecv

        def begin(self):
            src = self.part.at[pl.ds(al(3200 * other, 16), 3200), :]
            k = self.base
            push(src, self.sib, rsend.at[k], rrecv.at[k], {"seq": other})

        def begin_wait(self):
            k = self.base
            copy(self.sib, self.sib, rsend.at[k], rrecv.at[k], {"seq": other}).wait_recv()

        def pair(self, dz, lo, size):
            d = lax.rem(z + dz + NZ, NZ)
            mine = self.part[pl.ds(al(3200 * core + BLK * d + lo, 16), size), :]
            theirs = self.sib[pl.ds(al(BLK * d + lo, 16), size), :]
            return mine.astype(F32) + theirs.astype(F32)

        def go(self, s, lo, size):
            rows = pl.ds(lo, size)
            k = self.base + 1 + s
            push(self.psend.at[s, rows, :], self.precv.at[s, rows, :], rsend.at[k], rrecv.at[k],
                 {"tensor": zplus})

        def go_minus(self, s, lo, size):
            rows = pl.ds(lo, size)
            k = self.base + 5 + s
            push(self.msend.at[s, rows, :], self.mrecv.at[s, rows, :], rsend.at[k], rrecv.at[k],
                 {"tensor": zminus})

        def wait_plus(self, s, lo, size):
            ref = self.precv.at[s, pl.ds(lo, size), :]
            k = self.base + 1 + s
            copy(ref, ref, rsend.at[k], rrecv.at[k], {"tensor": zplus}).wait_recv()

        def wait_minus(self, s, lo, size):
            ref = self.mrecv.at[s, pl.ds(lo, size), :]
            k = self.base + 5 + s
            copy(ref, ref, rsend.at[k], rrecv.at[k], {"tensor": zminus}).wait_recv()

        def s0(self):
            rest = BLK - HALF_A
            self.psend[0, 0:HALF_A, :] = self.pair(4, 0, HALF_A).astype(BF16)
            self.go(0, 0, HALF_A)
            self.msend[0, HALF_A:BLK, :] = self.pair(4, HALF_A, rest).astype(BF16)
            self.go_minus(0, HALF_A, rest)

        def s1(self):
            rest = BLK - HALF_A
            self.psend[1, HALF_A:BLK, :] = self.pair(3, HALF_A, rest).astype(BF16)
            self.msend[1, 0:HALF_A, :] = self.pair(-3, 0, HALF_A).astype(BF16)
            self.wait_plus(0, 0, HALF_A)
            got = self.precv[0, 0:HALF_A, :].astype(F32)
            self.psend[1, 0:HALF_A, :] = (self.pair(3, 0, HALF_A) + got).astype(BF16)
            self.go(1, 0, BLK)
            self.wait_minus(0, HALF_A, rest)
            got = self.mrecv[0, HALF_A:BLK, :].astype(F32)
            self.msend[1, HALF_A:BLK, :] = (self.pair(-3, HALF_A, rest) + got).astype(BF16)
            self.go_minus(1, 0, BLK)

        def step(self, s):
            self.wait_plus(s - 1, 0, BLK)
            got = self.precv[s - 1].astype(F32)
            self.psend[s] = (self.pair(4 - s, 0, BLK) + got).astype(BF16)
            self.go(s, 0, BLK)
            self.wait_minus(s - 1, 0, BLK)
            got = self.mrecv[s - 1].astype(F32)
            self.msend[s] = (self.pair(s - 4, 0, BLK) + got).astype(BF16)
            self.go_minus(s, 0, BLK)

        def end(self):
            self.wait_plus(3, 0, BLK)
            self.wait_minus(3, 0, BLK)
            return (
                self.pair(0, 0, BLK)
                + self.precv[3].astype(F32)
                + self.mrecv[3].astype(F32)
            )

    sum_r = Scatter(0, part_r, sib_r, psend_r, precv_r, msend_r, mrecv_r)
    sum_s = Scatter(1, part_s, sib_s, psend_s, precv_s, msend_s, mrecv_s)

    def unpack_strip(words, scale_rows, store):
        w = words.astype(I32) ^ 0x88888
        for k in range(5):
            shift = 28 - 4 * k
            code = lax.shift_right_arithmetic(lax.shift_left(w, I32(shift)), I32(28))
            store(k, (code.astype(F32) * scale_rows[k]).astype(BF16))

    def unpack_gu(codes, scales, m, strip):
        b = strip // 8
        inner = lax.rem(strip, 8) * 16
        rows = [scales[m, pl.ds(5 * b + k, 1), :] for k in range(5)]

        def store(k, value):
            weights[m, pl.ds(al((5 * b + k) * 128 + inner, 16), 16), :] = value

        unpack_strip(codes[m, pl.ds(al(strip * 16, 16), 16), :], rows, store)

    def unpack_routed(b):
        local_gu[b].wait()

        def one(i, _):
            unpack_gu(rgu, gu_scales, i // 8, 8 * b + lax.rem(i, 8))
            return 0

        lax.fori_loop(0, 16, one, 0)

    def unpack_shared(piece, r):
        for da, db in piece.arrived(r):
            ee = piece.block(da, db)

            def one(i, _):
                unpack_gu(gu_all, sgu_scales, piece.piece, 5 * ee + i)
                return 0

            lax.fori_loop(0, 5, one, 0)

    def transpose_in(src, dst):
        def one(i, _):
            at = al(i * 256, 256)
            dst[:, pl.ds(at, 256)] = src[pl.ds(at, 256), :].T
            return 0

        lax.fori_loop(0, 25, one, 0)

    def hidden_units(rows, x, target):
        zero = jnp.zeros((rows, HID), F32)
        acc_g[0:rows, :] = zero
        acc_u[0:rows, :] = zero

        def one(i, _):
            at = pl.ds(al(i * 640, 640), 640)
            xk = x[:, at]
            acc_g[0:rows, :] += jnp.dot(xk, weights[0, at, :], preferred_element_type=F32)
            acc_u[0:rows, :] += jnp.dot(xk, weights[1, at, :], preferred_element_type=F32)
            return 0

        lax.fori_loop(0, 10, one, 0)
        g = acc_g[0:rows, :]
        target[...] = (g / (1.0 + jnp.exp(-g)) * acc_u[0:rows, :]).astype(BF16)

    def down(words_of, scales, h, target, lo, hi):
        def one(j, _):
            cols = pl.ds(al(j * 640, 640), 640)

            def strip(i, _):
                rows = [scales[pl.ds(k, 1), cols] for k in range(5)]

                def store(k, value):
                    wdown[pl.ds(al(k * 128 + i * 16, 16), 16), :] = value

                unpack_strip(words_of(i, j), rows, store)
                return 0

            lax.fori_loop(0, 8, strip, 0)
            y = jnp.dot(h[...], wdown[...], preferred_element_type=F32).astype(BF16)
            target[cols, :] = y.T
            return 0

        lax.fori_loop(lo, hi, one, 0)

    local_own.wait()
    gate.r0()
    up.r0()

    expert_row = ids[...]
    onehot = (lax.broadcasted_iota(I32, (16, TOK), 0) == expert_row).astype(F32)
    upto = (
        lax.broadcasted_iota(I32, (TOK, TOK), 0) <= lax.broadcasted_iota(I32, (TOK, TOK), 1)
    ).astype(BF16)
    counted = jnp.dot(onehot.astype(BF16), upto, preferred_element_type=F32)
    rank = jnp.sum(counted * onehot, axis=0, keepdims=True) - 1.0
    slot = expert_row.astype(F32) * 16.0 + rank
    chosen = lax.broadcasted_iota(I32, (SLOTS, TOK), 0).astype(F32) == slot
    select[...] = chosen.astype(F32).astype(BF16)
    tok = tokens[...]
    disp[...] = jnp.dot(select[...], tok, preferred_element_type=F32).astype(BF16)

    def a2a(src, dst, k):
        def one(i, _):
            to = lax.rem(exp + i, 16)
            copy(
                src.at[pl.ds(al(16 * to, 16), 16), :],
                dst.at[pl.ds(al(16 * exp, 16), 16), :],
                asend.at[k],
                arecv.at[k],
                {"expert": to},
            ).start()
            return 0

        lax.fori_loop(1, 16, one, 0)
        mine = pl.ds(al(16 * exp, 16), 16)
        dst[mine, :] = src[mine, :]

    def a2a_wait(dst, k):
        ref = dst.at[pl.ds(0, 240), :]
        copy(ref, ref, asend.at[k], arecv.at[k], {"seq": other}).wait_recv()

    def a2a_end(src, k):
        ref = src.at[pl.ds(0, 240), :]
        copy(ref, ref, asend.at[k], arecv.at[k], {"seq": other}).wait_send()

    own_rows = pl.ds(al(3200 * core + BLK * z, 16), BLK)
    a2a(disp, disp_in, 0)
    tk_t[own_rows, :] = tok.T
    toks.r0()
    dn_all[pl.ds(al(400 * exp, 8), 400), :] = sdn_codes[...].T

    unpack_routed(0)
    unpack_routed(1)
    a2a_wait(disp_in, 0)
    xs_t[own_rows, :] = disp_in[...].T
    slots.r0()

    unpack_routed(2)
    toks.step(1)
    unpack_routed(3)
    gate.r1()
    up.r1()
    unpack_routed(4)
    slots.step(1)
    unpack_routed(5)
    unpack_routed(6)
    toks.step(2)
    unpack_routed(7)
    slots.step(2)
    unpack_routed(8)
    unpack_routed(9)
    slots.step(3)
    toks.step(3)
    gate.r2()
    up.r2()
    down_a.r0()
    down_b.r0()
    slots.last()
    transpose_in(xs_t, xs)
    hidden_units(SLOTS, xs, hidden)
    toks.last()

    local_dn.wait()

    def routed_words(i, j):
        return rdn[pl.ds(al(i * 16, 16), 16), pl.ds(al(j * 640, 640), 640)]

    down(routed_words, dn_scales, hidden, part_r, 0, 10)
    sum_r.begin()
    for r in (0, 1):
        unpack_shared(gate, r)
        unpack_shared(up, r)
    sum_r.begin_wait()
    sum_r.s0()
    unpack_shared(gate, 2)
    unpack_shared(up, 2)
    gate.r3()
    up.r3()
    down_a.r1()
    down_b.r1()
    sum_r.s1()
    unpack_shared(gate, 3)
    unpack_shared(up, 3)
    sum_r.step(2)
    gate.r4()
    up.r4()
    down_a.r2()
    down_b.r2()
    unpack_shared(gate, 4)
    unpack_shared(up, 4)
    transpose_in(tk_t, tk)
    hidden_units(TOK, tk, hidden_sh)
    sum_r.step(3)
    down_a.r3()
    down_b.r3()
    down_a.r4()
    down_b.r4()
    back[...] = sum_r.end().astype(BF16).T
    a2a(back, back_in, 1)

    def shared_words_at(j):
        rows = pl.ds(al(j * 640, 640), 640)
        rdn[:, rows] = dn_all[rows, :].T

    def turn(j, _):
        shared_words_at(j)
        return 0

    lax.fori_loop(0, 10, turn, 0)
    down(routed_words, sdn_scales, hidden_sh, part_s, 0, 10)
    sum_s.begin()
    sum_s.begin_wait()
    sum_s.s0()
    sum_s.s1()
    sum_s.step(2)
    sum_s.step(3)
    a2a_wait(back_in, 1)
    routed = lax.dot_general(
        select[...], back_in[...], (((0,), (0,)), ((), ())), preferred_element_type=F32
    )
    diag = lax.broadcasted_iota(I32, (TOK, TOK), 0) == lax.broadcasted_iota(I32, (TOK, TOK), 1)
    factor = jnp.sum(jnp.where(diag, gate_w[...], 0.0), axis=1, keepdims=True)
    shared = sum_s.end().T
    out[...] = (shared + factor * routed).astype(BF16)

    a2a_end(disp, 0)
    a2a_end(back, 1)
    for cp in sent:
        cp.wait_send()


def shards(
    tokens,
    expert_ids,
    gate_weights,
    gate_up_codes,
    gate_up_scales,
    down_codes,
    down_scales,
    shared_gate_up_codes,
    shared_gate_up_scales,
    shared_down_codes,
    shared_down_scales,
):
    vmem = pl.BlockSpec(memory_space=pltpu.VMEM)
    hbm = pl.BlockSpec(memory_space=pl.ANY)
    V = pltpu.VMEM
    S = pltpu.SemaphoreType.DMA
    return pl.pallas_call(
        kernel,
        out_shape=jax.ShapeDtypeStruct((TOK, BLK), BF16),
        in_specs=[vmem, vmem, vmem, hbm, vmem, hbm, vmem, hbm, vmem, vmem, vmem],
        out_specs=vmem,
        scratch_shapes=[
            V((2, 1280, HID), F32),
            V((128, D), F32),
            V((2, 1280, HID), F32),
            V((D, 128), F32),
            V((2, D, HID), BF16),
            V((HID, HID), BF16),
            V((D, SLOTS), BF16),
            V((SLOTS, D), BF16),
            V((D, TOK), BF16),
            V((TOK, D), BF16),
            V((SLOTS, HID), F32),
            V((SLOTS, HID), F32),
            V((SLOTS, HID), BF16),
            V((TOK, HID), BF16),
            V((D, SLOTS), BF16),
            V((D, TOK), BF16),
            V((3200, SLOTS), BF16),
            V((3200, TOK), BF16),
            V((4, BLK, SLOTS), BF16),
            V((4, BLK, SLOTS), BF16),
            V((4, BLK, SLOTS), BF16),
            V((4, BLK, SLOTS), BF16),
            V((4, BLK, TOK), BF16),
            V((4, BLK, TOK), BF16),
            V((4, BLK, TOK), BF16),
            V((4, BLK, TOK), BF16),
            V((SLOTS, TOK), BF16),
            V((SLOTS, BLK), BF16),
            V((SLOTS, BLK), BF16),
            V((SLOTS, BLK), BF16),
            V((SLOTS, BLK), BF16),
            V((8, 128), F32),
            V((8, 128), F32),
            S((80,)),
            S((80,)),
            S((34,)),
            S((34,)),
            S((2,)),
            S((2,)),
            S((18,)),
            S((18,)),
            S((12,)),
        ],
        compiler_params=pltpu.CompilerParams(
            collective_id=0, has_side_effects=True, vmem_limit_bytes=64 * 1024 * 1024 - 65536
        ),
    )(
        tokens,
        expert_ids.reshape(1, TOK),
        gate_weights.reshape(1, TOK),
        gate_up_codes[0],
        gate_up_scales[0],
        down_codes[0],
        down_scales[0],
        shared_gate_up_codes,
        shared_gate_up_scales,
        shared_down_codes,
        shared_down_scales,
    )


def solution(mesh):
    placed = (
        P("expert", ("seq", "tensor")),
        P("expert"),
        P("expert"),
        P("expert", None, None, ("seq", "tensor")),
        P("expert", None, None, ("seq", "tensor")),
        P("expert", ("seq", "tensor"), None),
        P("expert", ("seq", "tensor"), None),
        P(None, "expert", ("seq", "tensor")),
        P(None, None, ("seq", "tensor")),
        P(("seq", "tensor"), "expert"),
        P(("seq", "tensor"), None),
    )
    return jax.shard_map(
        shards,
        mesh=mesh,
        in_specs=placed,
        out_specs=P("expert", ("seq", "tensor")),
        check_vma=False,
    )
```

```python
import jax
import jax.numpy as jnp
from jax import lax
from jax.experimental import pallas as pl
from jax.experimental.pallas import tpu as pltpu
from jax.sharding import PartitionSpec as P

MESH = pl.DeviceIdType.MESH
F32 = jnp.float32
BF16 = jnp.bfloat16
I32 = jnp.int32

D = 6400
HID = 640
SLOTS = 256
TOK = 128
BLK = 400
PARTS = ((0, 208), (208, 192), (0, 400))
NZ = 8


def al(value, multiple):
    return pl.multiple_of(value, multiple)


def pick(j, values):
    chosen = values[0]
    for k in range(1, len(values)):
        chosen = lax.select(j == k, values[k], chosen)
    return chosen


def kernel(
    tokens,
    ids_in,
    gate_in,
    gu_codes,
    gu_scales_in,
    dn_codes,
    dn_scales_in,
    sgu_codes,
    sgu_scales_in,
    sdn_codes,
    sdn_scales_in,
    out,
    ids,
    gate_w,
    gu_scales,
    dn_scales,
    sgu_scales,
    sdn_scales,
    scale_rows,
    scale_cols,
    rgu,
    rdn,
    rdn_t,
    gu_all,
    dn_all,
    weights,
    wshard,
    wdown,
    xs_t,
    tk_t,
    xperm,
    acc_r,
    acc_s,
    hid_r,
    hid_s,
    part_r,
    part_s,
    sib_r,
    sib_s,
    precv_r,
    mrecv_r,
    precv_s,
    mrecv_s,
    select,
    disp,
    disp_in,
    back,
    back_in,
    wsend,
    wrecv,
    zsend,
    zrecv,
    asend,
    arecv,
    rsend,
    rrecv,
    lsem,
):
    core = lax.axis_index("seq")
    exp = lax.axis_index("expert")
    z = lax.axis_index("tensor")
    ex = exp // 4
    ey = lax.rem(exp, 4)
    other = 1 - core
    zplus = lax.rem(z + 1, NZ)
    zminus = lax.rem(z + NZ - 1, NZ)

    barrier = pltpu.get_barrier_semaphore()

    def greet(k, _):
        pl.semaphore_signal(
            barrier, inc=1, device_id={"expert": lax.rem(exp + k, 16)}, device_id_type=MESH
        )
        return 0

    pl.semaphore_signal(barrier, inc=1, device_id={"seq": other}, device_id_type=MESH)
    pl.semaphore_signal(barrier, inc=1, device_id={"tensor": zplus}, device_id_type=MESH)
    pl.semaphore_signal(barrier, inc=1, device_id={"tensor": zminus}, device_id_type=MESH)
    lax.fori_loop(1, 16, greet, 0)

    def load(src, dst, k):
        cp = pltpu.make_async_copy(src, dst, lsem.at[k])
        cp.start()
        return cp

    own_rows = pl.ds(al(3200 * core + BLK * z, 16), BLK)
    dn_rows = pl.ds(al(BLK * exp, 16), BLK)
    local_tok = load(tokens, tk_t.at[own_rows, :], 0)
    local_ids = load(ids_in, ids, 1)
    local_gate = load(gate_in, gate_w, 2)
    local_sgu = load(sgu_codes, gu_all.at[:, pl.ds(al(80 * exp, 8), 80), :], 3)
    local_sdn = load(sdn_codes, dn_all.at[dn_rows, :], 4)
    local_gs = load(gu_scales_in, gu_scales, 5)
    local_gu = []
    for b in range(10):
        rows = pl.ds(128 * b, 128)
        local_gu.append(load(gu_codes.at[:, rows, :], rgu.at[:, rows, :], 10 + b))
    local_dn = load(dn_codes, rdn, 6)
    local_ds = load(dn_scales_in, dn_scales, 7)
    local_ss = load(sgu_scales_in, sgu_scales, 8)
    local_sds = load(sdn_scales_in, sdn_scales, 9)

    sent = []

    def copy(src, dst, ssem, rsem, device):
        return pltpu.make_async_remote_copy(
            src_ref=src,
            dst_ref=dst,
            send_sem=ssem,
            recv_sem=rsem,
            device_id=device,
            device_id_type=MESH,
        )

    def push(src, dst, ssem, rsem, device):
        cp = copy(src, dst, ssem, rsem, device)
        cp.start()
        sent.append(cp)

    def region(piece, ee, half):
        if piece < 2:
            off, size = ((0, 80), (0, 40), (40, 40))[half]
            return gu_all.at[piece, pl.ds(al(80 * ee + off, 8), size), :]
        base = 200 * (piece - 2)
        off, size = ((0, 200), (0, 104), (104, 96))[half]
        return dn_all.at[pl.ds(al(400 * ee + (base + off), 8), size), :]

    class Piece:
        def __init__(self, piece):
            self.piece = piece
            self.by_x = piece % 2 == 0
            self.a = ex if self.by_x else ey
            self.b = ey if self.by_x else ex

        def block(self, da, db):
            a = lax.rem(self.a + da + 4, 4)
            b = lax.rem(self.b + db + 4, 4)
            return a * 4 + b if self.by_x else b * 4 + a

        def send(self, sem, da, db, half, step_a, step_b):
            ref = region(self.piece, self.block(da, db), half)
            s = 20 * self.piece + sem
            push(ref, ref, wsend.at[s], wrecv.at[s], {"expert": self.block(step_a, step_b)})

        def wait(self, sem, da, db, half):
            ref = region(self.piece, self.block(da, db), half)
            s = 20 * self.piece + sem
            copy(ref, ref, wsend.at[s], wrecv.at[s], {"expert": self.block(1, 0)}).wait_recv()

        def stage2(self, q, da):
            self.send(4 + 4 * q, da, 0, 0, 0, 1)
            self.send(5 + 4 * q, da, 0, 0, 0, -1)

        def stage2_forward(self, q, da):
            self.wait(4 + 4 * q, da, -1, 0)
            self.send(6 + 4 * q, da, -1, 1, 0, 1)
            self.wait(5 + 4 * q, da, 1, 0)
            self.send(7 + 4 * q, da, 1, 2, 0, -1)

        def stage2_end(self, q, da):
            self.wait(6 + 4 * q, da, 2, 1)
            self.wait(7 + 4 * q, da, 2, 2)

        def r0(self):
            self.send(0, 0, 0, 0, 1, 0)
            self.send(1, 0, 0, 0, -1, 0)
            self.stage2(0, 0)

        def r1(self):
            self.wait(0, -1, 0, 0)
            self.send(2, -1, 0, 1, 1, 0)
            self.stage2(1, -1)
            self.wait(1, 1, 0, 0)
            self.send(3, 1, 0, 2, -1, 0)
            self.stage2(2, 1)
            self.stage2_forward(0, 0)

        def r2(self):
            self.wait(2, 2, 0, 1)
            self.wait(3, 2, 0, 2)
            self.stage2(3, 2)
            self.stage2_forward(1, -1)
            self.stage2_forward(2, 1)
            self.stage2_end(0, 0)

        def r3(self):
            self.stage2_forward(3, 2)
            self.stage2_end(1, -1)
            self.stage2_end(2, 1)

        def r4(self):
            self.stage2_end(3, 2)

        def arrived(self, r):
            places = (
                ((0, 0),),
                ((-1, 0), (1, 0), (0, -1), (0, 1)),
                ((2, 0), (0, 2), (-1, -1), (-1, 1), (1, -1), (1, 1)),
                ((2, -1), (2, 1), (-1, 2), (1, 2)),
                ((2, 2),),
            )[r]
            return [self.block(da, db) for da, db in places]

    gate, up, down_a, down_b = (Piece(i) for i in range(4))

    def block_of(c, dz):
        return NZ * c + lax.rem(z + dz + NZ, NZ)

    class Gather:
        def __init__(self, ref, which):
            self.ref = ref
            self.base = 32 * which

        def rows(self, c, dz, part):
            off, size = PARTS[part]
            return self.ref.at[pl.ds(al(BLK * block_of(c, dz) + off, 16), size), :]

        def ring(self, up_way, r, part):
            ref = self.rows(core, -r if up_way else r, part)
            k = self.base + (0 if up_way else 8) + 2 * r + part
            to = zplus if up_way else zminus
            push(ref, ref, zsend.at[k], zrecv.at[k], {"tensor": to})

        def sibling(self, dz, part):
            ref = self.rows(core, dz, part)
            k = self.base + 16 + 2 * (dz % NZ) + part
            push(ref, ref, zsend.at[k], zrecv.at[k], {"seq": other})

        def ring_wait(self, up_way, r, part):
            ref = self.rows(core, -r if up_way else r, part)
            k = self.base + (0 if up_way else 8) + 2 * (r - 1) + part
            copy(ref, ref, zsend.at[k], zrecv.at[k], {"tensor": zplus}).wait_recv()

        def sibling_wait(self, dz):
            for part in (0, 1):
                ref = self.rows(other, dz, part)
                k = self.base + 16 + 2 * (dz % NZ) + part
                copy(ref, ref, zsend.at[k], zrecv.at[k], {"seq": other}).wait_recv()

        def r0(self):
            for part in (0, 1):
                self.ring(True, 0, part)
                self.ring(False, 0, part)
            for part in (0, 1):
                self.sibling(0, part)

        def step(self, r):
            for part in (0, 1):
                for up_way in (True, False):
                    long_way = (part == 0) == up_way
                    if r == 4 and not long_way:
                        continue
                    self.ring_wait(up_way, r, part)
                    if r <= (3 if long_way else 2):
                        self.ring(up_way, r, part)
                    self.sibling(-r if up_way else r, part)

    slots = Gather(xs_t, 0)
    toks = Gather(tk_t, 1)

    class Scatter:
        def __init__(self, which, part, sib, precv, mrecv):
            self.base = 24 * which
            self.part, self.sib = part, sib
            self.recv = (precv, mrecv)

        def to_sibling(self, d):
            rows = pl.ds(al(BLK * (NZ * other + d), 16), BLK)
            k = self.base + d
            push(
                self.part.at[rows, :],
                self.sib.at[pl.ds(al(BLK * d, 16), BLK), :],
                rsend.at[k],
                rrecv.at[k],
                {"seq": other},
            )

        def sibling_wait(self, d):
            ref = self.sib.at[pl.ds(al(BLK * d, 16), BLK), :]
            k = self.base + d
            copy(ref, ref, rsend.at[k], rrecv.at[k], {"seq": other}).wait_recv()

        def pair(self, d, part):
            lo, size = PARTS[part]
            mine = self.part[pl.ds(al(BLK * (NZ * core + d) + lo, 16), size), :]
            theirs = self.sib[pl.ds(al(BLK * d + lo, 16), size), :]
            return mine.astype(F32) + theirs.astype(F32)

        def slot(self, way, s, part):
            lo, size = PARTS[part]
            return self.recv[way].at[s, pl.ds(lo, size), :]

        def wait(self, way, s, part):
            ref = self.slot(way, s, part)
            k = self.base + 8 + 8 * way + 2 * s + part
            copy(ref, ref, rsend.at[k], rrecv.at[k], {"tensor": zplus}).wait_recv()

        def message(self, way, s, part):
            lo, size = PARTS[part]
            d = lax.rem(z + (4 - s if way == 0 else s - 4) + NZ, NZ)
            value = self.pair(d, part)
            if s > (0 if way == part else 1):
                self.wait(way, s - 1, part)
                value = value + self.recv[way][s - 1, pl.ds(lo, size), :].astype(F32)
            rows = pl.ds(al(BLK * (NZ * core + d) + lo, 16), size)
            self.part[rows, :] = value.astype(BF16)
            k = self.base + 8 + 8 * way + 2 * s + part
            push(
                self.part.at[rows, :],
                self.slot(way, s, part),
                rsend.at[k],
                rrecv.at[k],
                {"tensor": zplus if way == 0 else zminus},
            )

        def step(self, s):
            if s == 0:
                self.message(0, 0, 0)
                self.message(1, 0, 1)
                return
            if s == 1:
                self.message(0, 1, 1)
                self.message(1, 1, 0)
                self.message(0, 1, 0)
                self.message(1, 1, 1)
                return
            for part in (0, 1):
                self.message(part, s, 1 - part)
            for part in (0, 1):
                self.message(part, s, part)

        def end(self):
            for way in (0, 1):
                for part in (0, 1):
                    self.wait(way, 3, part)
            return (
                self.pair(z, 2)
                + self.recv[0][3].astype(F32)
                + self.recv[1][3].astype(F32)
            )

    sum_r = Scatter(0, part_r, sib_r, precv_r, mrecv_r)
    sum_s = Scatter(1, part_s, sib_s, precv_s, mrecv_s)

    def digits(words, scale_of, store):
        w = words.astype(I32) ^ 0x88888
        for k in range(5):
            code = lax.shift_right_arithmetic(lax.shift_left(w, I32(28 - 4 * k)), I32(28))
            store(k, (code.astype(F32) * scale_of(k)).astype(BF16))

    def unpack_routed(b):
        local_gu[b].wait()

        def one(i, _):
            inner = i * 16
            for m in (0, 1):

                def scale_of(k):
                    return gu_scales[5 * b + k, pl.ds(m, 1), :]

                def store(k, value):
                    rows = pl.ds(al((5 * b + k) * 128 + inner, 16), 16)
                    weights[rows, m * HID : (m + 1) * HID] = value

                digits(rgu[m, pl.ds(al(128 * b + inner, 16), 16), :], scale_of, store)
            return 0

        lax.fori_loop(0, 8, one, 0)

    def routed_blocks(blocks):
        def one(j, _):
            rows = pl.ds(al(BLK * pick(j, blocks), 16), BLK)
            acc_r[...] += jnp.dot(
                xs_t[rows, :].T, weights[rows, :], preferred_element_type=F32
            )
            return 0

        lax.fori_loop(0, len(blocks), one, 0)

    def shared_shards(shards_in):
        def one(j, _):
            ee = pick(j, shards_in)

            def strip(i, _):
                s = 5 * ee + i
                b = s // 8
                inner = lax.rem(s, 8) * 16
                at = i * 16
                for k in range(5):
                    xperm[pl.ds(al(k * 80 + at, 16), 16), :] = tk_t[
                        pl.ds(al((5 * b + k) * 128 + inner, 16), 16), :
                    ]
                for m in (0, 1):

                    def scale_of(k):
                        return sgu_scales[5 * b + k, pl.ds(m, 1), :]

                    def store(k, value):
                        rows = pl.ds(al(k * 80 + at, 16), 16)
                        wshard[rows, m * HID : (m + 1) * HID] = value

                    digits(gu_all[m, pl.ds(al(s * 16, 16), 16), :], scale_of, store)
                return 0

            lax.fori_loop(0, 5, strip, 0)
            acc_s[...] += jnp.dot(xperm[...].T, wshard[...], preferred_element_type=F32)
            return 0

        lax.fori_loop(0, len(shards_in), one, 0)

    def activate(acc, target):
        g = acc[:, 0:HID]
        h = g / (1.0 + jnp.exp(-g)) * acc[:, HID : 2 * HID]
        target[...] = h.astype(BF16).T

    def down_blocks(words, lane, hid, target, blocks, then=None):
        def one(j, _):
            i = pick(j, blocks)

            def strip(q, _):
                rows = pl.ds(al(BLK * i + q * 80, 16), 80)

                def scale_of(k):
                    return scale_cols[rows, lane + k : lane + k + 1]

                def store(k, value):
                    wdown[pl.ds(al(q * 80, 16), 80), k * 128 : (k + 1) * 128] = value

                digits(words[rows, :], scale_of, store)
                return 0

            lax.fori_loop(0, 5, strip, 0)
            y = jnp.dot(wdown[...], hid[...], preferred_element_type=F32)
            target[pl.ds(al(BLK * i, 16), BLK), :] = y.astype(BF16)
            return 0

        lax.fori_loop(0, len(blocks), one, 0)

    local_tok.wait()
    local_ids.wait()
    expert_row = ids[...]
    onehot = (lax.broadcasted_iota(I32, (16, TOK), 0) == expert_row).astype(F32)
    upto = (
        lax.broadcasted_iota(I32, (TOK, TOK), 0) <= lax.broadcasted_iota(I32, (TOK, TOK), 1)
    ).astype(BF16)
    counted = jnp.dot(onehot.astype(BF16), upto, preferred_element_type=F32)
    rank = jnp.sum(counted * onehot, axis=0, keepdims=True) - 1.0
    slot = expert_row.astype(F32) * 16.0 + rank
    chosen = lax.broadcasted_iota(I32, (SLOTS, TOK), 0).astype(F32) == slot
    select[...] = chosen.astype(F32).astype(BF16)
    disp[...] = lax.dot_general(
        select[...], tk_t[own_rows, :], (((1,), (1,)), ((), ())), preferred_element_type=F32
    ).astype(BF16)
    local_sgu.wait()
    local_sdn.wait()
    local_gs.wait()

    def a2a(src, dst, k):
        def one(i, _):
            to = lax.rem(exp + i, 16)
            copy(
                src.at[pl.ds(al(16 * to, 16), 16), :],
                dst.at[pl.ds(al(16 * exp, 16), 16), :],
                asend.at[k],
                arecv.at[k],
                {"expert": to},
            ).start()
            return 0

        lax.fori_loop(1, 16, one, 0)
        mine = pl.ds(al(16 * exp, 16), 16)
        dst[mine, :] = src[mine, :]

    def a2a_wait(dst, k):
        ref = dst.at[pl.ds(0, 240), :]
        copy(ref, ref, asend.at[k], arecv.at[k], {"seq": other}).wait_recv()

    def a2a_end(src, k):
        ref = src.at[pl.ds(0, 240), :]
        copy(ref, ref, asend.at[k], arecv.at[k], {"seq": other}).wait_send()

    pl.semaphore_wait(barrier, 18)

    a2a(disp, disp_in, 0)
    toks.r0()
    gate.r0()
    up.r0()
    acc_r[...] = jnp.zeros(acc_r.shape, F32)
    acc_s[...] = jnp.zeros(acc_s.shape, F32)
    unpack_routed(0)
    unpack_routed(1)
    unpack_routed(2)
    toks.step(1)
    unpack_routed(3)
    unpack_routed(4)
    toks.step(2)
    unpack_routed(5)
    a2a_wait(disp_in, 0)
    xs_t[own_rows, :] = disp_in[...].T
    slots.r0()
    unpack_routed(6)
    toks.step(3)
    unpack_routed(7)
    toks.step(4)
    unpack_routed(8)
    unpack_routed(9)

    local_ds.wait()
    local_sds.wait()
    local_dn.wait()
    local_ss.wait()
    for k in range(5):
        scale_rows[k : k + 1, :] = dn_scales[k, :, :]
    scale_rows[8:13, :] = sdn_scales[...]

    def turn(j, _):
        at = pl.ds(al(j * 128, 128), 128)
        scale_cols[at, 0:16] = scale_rows[:, at].T
        rdn_t[at, :] = rdn[:, at].T
        return 0

    lax.fori_loop(0, 50, turn, 0)
    slots.step(1)
    gate.r1()
    up.r1()
    down_a.r0()
    down_b.r0()
    slots.sibling_wait(0)
    routed_blocks([block_of(core, 0), block_of(other, 0)])
    for dz in (0, 1, -1, 2, -2, 3, -3, 4):
        toks.sibling_wait(dz)
    shared_shards(gate.arrived(0))
    slots.step(2)
    routed_blocks([block_of(core, 1), block_of(core, -1)])
    shared_shards(gate.arrived(1))
    slots.step(3)
    slots.sibling_wait(1)
    slots.sibling_wait(-1)
    routed_blocks([block_of(c, dz) for c, dz in ((other, 1), (other, -1), (core, 2), (core, -2))])
    gate.r2()
    up.r2()
    slots.step(4)
    down_a.r1()
    down_b.r1()
    slots.sibling_wait(2)
    slots.sibling_wait(-2)
    routed_blocks([block_of(c, dz) for c, dz in ((other, 2), (other, -2), (core, 3), (core, -3))])
    slots.sibling_wait(3)
    slots.sibling_wait(-3)
    slots.sibling_wait(4)
    routed_blocks([block_of(c, dz) for c, dz in ((other, 3), (other, -3), (core, 4), (other, 4))])
    activate(acc_r, hid_r)

    def routed_down(offsets):
        blocks = []
        for dz in offsets:
            blocks += [block_of(other, dz), block_of(core, dz)]
        down_blocks(rdn_t, 0, hid_r, part_r, blocks)
        for dz in offsets:
            sum_r.to_sibling(lax.rem(z + dz + NZ, NZ))

    def routed_wait(offsets):
        for dz in offsets:
            sum_r.sibling_wait(lax.rem(z + dz + NZ, NZ))

    routed_down((4,))
    routed_down((3, -3))
    routed_wait((4,))
    sum_r.step(0)
    gate.r3()
    up.r3()
    routed_wait((3, -3))
    sum_r.step(1)
    down_a.r2()
    down_b.r2()
    routed_down((2, -2))
    shared_shards(gate.arrived(2)[0:2])
    routed_wait((2, -2))
    sum_r.step(2)
    gate.r4()
    up.r4()
    routed_down((1, -1))
    shared_shards(gate.arrived(2)[2:6])
    routed_wait((1, -1))
    sum_r.step(3)
    down_a.r3()
    down_b.r3()
    routed_down((0,))
    shared_shards(gate.arrived(3))
    routed_wait((0,))
    back[...] = sum_r.end().astype(BF16).T
    a2a(back, back_in, 1)
    shared_shards(gate.arrived(4))
    activate(acc_s, hid_s)
    down_a.r4()
    down_b.r4()

    def shared_down(blocks):
        down_blocks(dn_all, 8, hid_s, part_s, blocks)

    def shared_order(offsets):
        blocks = []
        for dz in offsets:
            blocks += [block_of(other, dz), block_of(core, dz)]
        shared_down(blocks)
        for dz in offsets:
            sum_s.to_sibling(lax.rem(z + dz + NZ, NZ))

    def shared_wait(offsets):
        for dz in offsets:
            sum_s.sibling_wait(lax.rem(z + dz + NZ, NZ))

    shared_order((4,))
    shared_order((3, -3))
    shared_wait((4,))
    sum_s.step(0)
    shared_wait((3, -3))
    sum_s.step(1)
    shared_order((2, -2))
    shared_wait((2, -2))
    sum_s.step(2)
    shared_order((1, -1))
    shared_wait((1, -1))
    sum_s.step(3)
    shared_order((0,))
    shared_wait((0,))
    a2a_wait(back_in, 1)
    local_gate.wait()
    routed = lax.dot_general(
        back_in[...], select[...], (((0,), (0,)), ((), ())), preferred_element_type=F32
    )
    out[...] = (sum_s.end() + gate_w[...] * routed).astype(BF16)

    a2a_end(disp, 0)
    a2a_end(back, 1)
    for cp in sent:
        cp.wait_send()


def shards(
    tokens,
    expert_ids,
    gate_weights,
    gate_up_codes,
    gate_up_scales,
    down_codes,
    down_scales,
    shared_gate_up_codes,
    shared_gate_up_scales,
    shared_down_codes,
    shared_down_scales,
):
    hbm = pl.BlockSpec(memory_space=pl.ANY)
    V = pltpu.VMEM
    S = pltpu.SemaphoreType.DMA
    return pl.pallas_call(
        kernel,
        out_shape=jax.ShapeDtypeStruct((BLK, TOK), BF16),
        in_specs=[hbm] * 11,
        out_specs=pl.BlockSpec(memory_space=pltpu.VMEM),
        scratch_shapes=[
            V((1, TOK), I32),
            V((1, TOK), F32),
            V((50, 2, HID), F32),
            V((5, 1, D), F32),
            V((50, 2, HID), F32),
            V((5, D), F32),
            V((16, D), F32),
            V((D, 16), F32),
            V((2, 1280, HID), F32),
            V((128, D), F32),
            V((D, 128), F32),
            V((2, 1280, HID), F32),
            V((D, 128), F32),
            V((D, 2 * HID), BF16),
            V((BLK, 2 * HID), BF16),
            V((BLK, HID), BF16),
            V((D, SLOTS), BF16),
            V((D, TOK), BF16),
            V((BLK, TOK), BF16),
            V((SLOTS, 2 * HID), F32),
            V((TOK, 2 * HID), F32),
            V((HID, SLOTS), BF16),
            V((HID, TOK), BF16),
            V((D, SLOTS), BF16),
            V((D, TOK), BF16),
            V((3200, SLOTS), BF16),
            V((3200, TOK), BF16),
            V((4, BLK, SLOTS), BF16),
            V((4, BLK, SLOTS), BF16),
            V((4, BLK, TOK), BF16),
            V((4, BLK, TOK), BF16),
            V((SLOTS, TOK), BF16),
            V((SLOTS, BLK), BF16),
            V((SLOTS, BLK), BF16),
            V((SLOTS, BLK), BF16),
            V((SLOTS, BLK), BF16),
            S((80,)),
            S((80,)),
            S((64,)),
            S((64,)),
            S((2,)),
            S((2,)),
            S((48,)),
            S((48,)),
            S((20,)),
        ],
        compiler_params=pltpu.CompilerParams(
            collective_id=0, has_side_effects=True, vmem_limit_bytes=64 * 1024 * 1024 - 65536
        ),
    )(
        tokens.T,
        expert_ids.reshape(1, TOK),
        gate_weights.reshape(1, TOK),
        gate_up_codes[0],
        jnp.transpose(gate_up_scales[0], (1, 0, 2)),
        down_codes[0],
        jnp.transpose(down_scales, (1, 0, 2)),
        shared_gate_up_codes,
        jnp.transpose(shared_gate_up_scales, (1, 0, 2)),
        shared_down_codes.T,
        shared_down_scales,
    ).T


def solution(mesh):
    placed = (
        P("expert", ("seq", "tensor")),
        P("expert"),
        P("expert"),
        P("expert", None, None, ("seq", "tensor")),
        P("expert", None, None, ("seq", "tensor")),
        P("expert", ("seq", "tensor"), None),
        P("expert", ("seq", "tensor"), None),
        P(None, "expert", ("seq", "tensor")),
        P(None, None, ("seq", "tensor")),
        P(("seq", "tensor"), "expert"),
        P(("seq", "tensor"), None),
    )
    return jax.shard_map(
        shards,
        mesh=mesh,
        in_specs=placed,
        out_specs=P("expert", ("seq", "tensor")),
        check_vma=False,
    )
```

```python
import jax
import jax.numpy as jnp
from jax import lax
from jax.experimental import pallas as pl
from jax.experimental.pallas import tpu as pltpu
from jax.sharding import PartitionSpec as P

MESH = pl.DeviceIdType.MESH
F32 = jnp.float32
BF16 = jnp.bfloat16
I32 = jnp.int32

D = 6400
HID = 640
SLOTS = 256
TOK = 128
BLK = 400
PARTS = ((0, 208), (208, 192), (0, 400))
NZ = 8


def al(value, multiple):
    return pl.multiple_of(value, multiple)


def pick(j, values):
    chosen = values[0]
    for k in range(1, len(values)):
        chosen = lax.select(j == k, values[k], chosen)
    return chosen


def kernel(
    tokens,
    ids_in,
    gate_in,
    gu_codes,
    gu_scales_in,
    dn_codes,
    dn_scales_in,
    sgu_codes,
    sgu_scales_in,
    sdn_codes,
    sdn_scales_in,
    out,
    ids,
    gate_w,
    gu_scales,
    dn_scales,
    sgu_scales,
    sdn_scales,
    scale_blocks,
    rgu,
    rdn,
    gu_all,
    dn_all,
    weights,
    wshard,
    wchunk,
    wblock,
    turned,
    xs_t,
    tk_t,
    xperm,
    acc_r,
    acc_s,
    hid_r,
    hid_s,
    part_r,
    part_s,
    sib_r,
    sib_s,
    precv_r,
    mrecv_r,
    precv_s,
    mrecv_s,
    select,
    disp,
    disp_in,
    back,
    back_in,
    wsend,
    wrecv,
    zsend,
    zrecv,
    asend,
    arecv,
    rsend,
    rrecv,
    lsem,
):
    core = lax.axis_index("seq")
    exp = lax.axis_index("expert")
    z = lax.axis_index("tensor")
    ex = exp // 4
    ey = lax.rem(exp, 4)
    other = 1 - core
    zplus = lax.rem(z + 1, NZ)
    zminus = lax.rem(z + NZ - 1, NZ)

    barrier = pltpu.get_barrier_semaphore()

    def greet(k, _):
        pl.semaphore_signal(
            barrier, inc=1, device_id={"expert": lax.rem(exp + k, 16)}, device_id_type=MESH
        )
        return 0

    pl.semaphore_signal(barrier, inc=1, device_id={"seq": other}, device_id_type=MESH)
    pl.semaphore_signal(barrier, inc=1, device_id={"tensor": zplus}, device_id_type=MESH)
    pl.semaphore_signal(barrier, inc=1, device_id={"tensor": zminus}, device_id_type=MESH)
    lax.fori_loop(1, 16, greet, 0)

    def load(src, dst, k):
        cp = pltpu.make_async_copy(src, dst, lsem.at[k])
        cp.start()
        return cp

    own_rows = pl.ds(al(3200 * core + BLK * z, 16), BLK)
    dn_rows = pl.ds(al(BLK * exp, 16), BLK)
    local_tok = load(tokens, tk_t.at[own_rows, :], 0)
    local_ids = load(ids_in, ids, 1)
    local_gate = load(gate_in, gate_w, 2)
    local_sgu = load(sgu_codes, gu_all.at[:, pl.ds(al(80 * exp, 8), 80), :], 3)
    local_sdn = load(sdn_codes, dn_all.at[dn_rows, :], 4)
    local_gs = load(gu_scales_in, gu_scales, 5)
    local_gu = []
    for b in range(10):
        rows = pl.ds(128 * b, 128)
        local_gu.append(load(gu_codes.at[:, rows, :], rgu.at[:, rows, :], 10 + b))
    local_dn = load(dn_codes, rdn, 6)
    local_ds = load(dn_scales_in, dn_scales, 7)
    local_ss = load(sgu_scales_in, sgu_scales, 8)
    local_sds = load(sdn_scales_in, sdn_scales, 9)

    sent = []

    def copy(src, dst, ssem, rsem, device):
        return pltpu.make_async_remote_copy(
            src_ref=src,
            dst_ref=dst,
            send_sem=ssem,
            recv_sem=rsem,
            device_id=device,
            device_id_type=MESH,
        )

    def push(src, dst, ssem, rsem, device):
        cp = copy(src, dst, ssem, rsem, device)
        cp.start()
        sent.append(cp)

    def region(piece, ee, half):
        if piece < 2:
            off, size = ((0, 80), (0, 40), (40, 40))[half]
            return gu_all.at[piece, pl.ds(al(80 * ee + off, 8), size), :]
        base = 200 * (piece - 2)
        off, size = ((0, 200), (0, 104), (104, 96))[half]
        return dn_all.at[pl.ds(al(400 * ee + (base + off), 8), size), :]

    class Piece:
        def __init__(self, piece):
            self.piece = piece
            self.by_x = piece % 2 == 0
            self.a = ex if self.by_x else ey
            self.b = ey if self.by_x else ex

        def block(self, da, db):
            a = lax.rem(self.a + da + 4, 4)
            b = lax.rem(self.b + db + 4, 4)
            return a * 4 + b if self.by_x else b * 4 + a

        def send(self, sem, da, db, half, step_a, step_b):
            ref = region(self.piece, self.block(da, db), half)
            s = 20 * self.piece + sem
            push(ref, ref, wsend.at[s], wrecv.at[s], {"expert": self.block(step_a, step_b)})

        def wait(self, sem, da, db, half):
            ref = region(self.piece, self.block(da, db), half)
            s = 20 * self.piece + sem
            copy(ref, ref, wsend.at[s], wrecv.at[s], {"expert": self.block(1, 0)}).wait_recv()

        def stage2(self, q, da):
            self.send(4 + 4 * q, da, 0, 0, 0, 1)
            self.send(5 + 4 * q, da, 0, 0, 0, -1)

        def stage2_forward(self, q, da):
            self.wait(4 + 4 * q, da, -1, 0)
            self.send(6 + 4 * q, da, -1, 1, 0, 1)
            self.wait(5 + 4 * q, da, 1, 0)
            self.send(7 + 4 * q, da, 1, 2, 0, -1)

        def stage2_end(self, q, da):
            self.wait(6 + 4 * q, da, 2, 1)
            self.wait(7 + 4 * q, da, 2, 2)

        def r0(self):
            self.send(0, 0, 0, 0, 1, 0)
            self.send(1, 0, 0, 0, -1, 0)
            self.stage2(0, 0)

        def r1(self):
            self.wait(0, -1, 0, 0)
            self.send(2, -1, 0, 1, 1, 0)
            self.stage2(1, -1)
            self.wait(1, 1, 0, 0)
            self.send(3, 1, 0, 2, -1, 0)
            self.stage2(2, 1)
            self.stage2_forward(0, 0)

        def r2(self):
            self.wait(2, 2, 0, 1)
            self.wait(3, 2, 0, 2)
            self.stage2(3, 2)
            self.stage2_forward(1, -1)
            self.stage2_forward(2, 1)
            self.stage2_end(0, 0)

        def r3(self):
            self.stage2_forward(3, 2)
            self.stage2_end(1, -1)
            self.stage2_end(2, 1)

        def r4(self):
            self.stage2_end(3, 2)

        def arrived(self, r):
            places = (
                ((0, 0),),
                ((-1, 0), (1, 0), (0, -1), (0, 1)),
                ((2, 0), (0, 2), (-1, -1), (-1, 1), (1, -1), (1, 1)),
                ((2, -1), (2, 1), (-1, 2), (1, 2)),
                ((2, 2),),
            )[r]
            return [self.block(da, db) for da, db in places]

    gate, up, down_a, down_b = (Piece(i) for i in range(4))

    def block_of(c, dz):
        return NZ * c + lax.rem(z + dz + NZ, NZ)

    class Gather:
        def __init__(self, ref, which):
            self.ref = ref
            self.base = 32 * which

        def rows(self, c, dz, part):
            off, size = PARTS[part]
            return self.ref.at[pl.ds(al(BLK * block_of(c, dz) + off, 16), size), :]

        def ring(self, up_way, r, part):
            ref = self.rows(core, -r if up_way else r, part)
            k = self.base + (0 if up_way else 8) + 2 * r + part
            to = zplus if up_way else zminus
            push(ref, ref, zsend.at[k], zrecv.at[k], {"tensor": to})

        def sibling(self, dz, part):
            ref = self.rows(core, dz, part)
            k = self.base + 16 + 2 * (dz % NZ) + part
            push(ref, ref, zsend.at[k], zrecv.at[k], {"seq": other})

        def ring_wait(self, up_way, r, part):
            ref = self.rows(core, -r if up_way else r, part)
            k = self.base + (0 if up_way else 8) + 2 * (r - 1) + part
            copy(ref, ref, zsend.at[k], zrecv.at[k], {"tensor": zplus}).wait_recv()

        def sibling_wait(self, dz):
            for part in (0, 1):
                ref = self.rows(other, dz, part)
                k = self.base + 16 + 2 * (dz % NZ) + part
                copy(ref, ref, zsend.at[k], zrecv.at[k], {"seq": other}).wait_recv()

        def start(self, long_way):
            part = 0 if long_way else 1
            self.ring(True, 0, part)
            self.ring(False, 0, 1 - part)
            self.sibling(0, part)

        def step(self, r, long_way):
            for up_way in (True, False):
                part = 0 if long_way == up_way else 1
                self.ring_wait(up_way, r, part)
                if r <= (3 if long_way else 2):
                    self.ring(up_way, r, part)
                self.sibling(-r if up_way else r, part)

    slots = Gather(xs_t, 0)
    toks = Gather(tk_t, 1)

    class Scatter:
        def __init__(self, which, part, sib, precv, mrecv):
            self.base = 24 * which
            self.part, self.sib = part, sib
            self.recv = (precv, mrecv)

        def sibling_copy(self, at, size, k):
            return copy(
                self.part.at[pl.ds(al(3200 * other + at, 16), size), :],
                self.sib.at[pl.ds(al(at, 16), size), :],
                rsend.at[self.base + k],
                rrecv.at[self.base + k],
                {"seq": other},
            )

        def sibling_wait(self, at, size, k):
            ref = self.sib.at[pl.ds(al(at, 16), size), :]
            k = self.base + k
            copy(ref, ref, rsend.at[k], rrecv.at[k], {"seq": other}).wait_recv()

        def pair(self, d, part):
            lo, size = PARTS[part]
            mine = self.part[pl.ds(al(BLK * (NZ * core + d) + lo, 16), size), :]
            theirs = self.sib[pl.ds(al(BLK * d + lo, 16), size), :]
            return mine.astype(F32) + theirs.astype(F32)

        def slot(self, way, s, part):
            lo, size = PARTS[part]
            return self.recv[way].at[s, pl.ds(lo, size), :]

        def wait(self, way, s, part):
            ref = self.slot(way, s, part)
            k = self.base + 8 + 8 * way + 2 * s + part
            copy(ref, ref, rsend.at[k], rrecv.at[k], {"tensor": zplus}).wait_recv()

        def message(self, way, s, part):
            lo, size = PARTS[part]
            d = lax.rem(z + (4 - s if way == 0 else s - 4) + NZ, NZ)
            value = self.pair(d, part)
            if s > (0 if way == part else 1):
                self.wait(way, s - 1, part)
                value = value + self.recv[way][s - 1, pl.ds(lo, size), :].astype(F32)
            rows = pl.ds(al(BLK * (NZ * core + d) + lo, 16), size)
            self.part[rows, :] = value.astype(BF16)
            k = self.base + 8 + 8 * way + 2 * s + part
            push(
                self.part.at[rows, :],
                self.slot(way, s, part),
                rsend.at[k],
                rrecv.at[k],
                {"tensor": zplus if way == 0 else zminus},
            )

        def long_step(self, s):
            self.message(0, s, 0)
            self.message(1, s, 1)

        def short_step(self, s):
            self.message(0, s, 1)
            self.message(1, s, 0)

        def end(self):
            for way in (0, 1):
                for part in (0, 1):
                    self.wait(way, 3, part)
            return (
                self.pair(z, 2)
                + self.recv[0][3].astype(F32)
                + self.recv[1][3].astype(F32)
            )

    sum_r = Scatter(0, part_r, sib_r, precv_r, mrecv_r)
    sum_s = Scatter(1, part_s, sib_s, precv_s, mrecv_s)

    def digits(words, scale_of, store):
        w = words.astype(I32) ^ 0x88888
        for k in range(5):
            code = lax.shift_right_arithmetic(lax.shift_left(w, I32(28 - 4 * k)), I32(28))
            store(k, (code.astype(F32) * scale_of(k)).astype(BF16))

    def unpack_routed(b):
        local_gu[b].wait()

        def one(i, _):
            inner = i * 16
            for m in (0, 1):

                def scale_of(k):
                    return gu_scales[5 * b + k, pl.ds(m, 1), :]

                def store(k, value):
                    rows = pl.ds(al((5 * b + k) * 128 + inner, 16), 16)
                    weights[rows, m * HID : (m + 1) * HID] = value

                digits(rgu[m, pl.ds(al(128 * b + inner, 16), 16), :], scale_of, store)
            return 0

        lax.fori_loop(0, 8, one, 0)

    def routed_blocks(blocks):
        def one(j, _):
            rows = pl.ds(al(BLK * pick(j, blocks), 16), BLK)
            acc_r[...] += jnp.dot(
                xs_t[rows, :].T, weights[rows, :], preferred_element_type=F32
            )
            return 0

        lax.fori_loop(0, len(blocks), one, 0)

    def shared_shards(shards_in):
        def one(j, _):
            ee = pick(j, shards_in)

            def strip(i, _):
                s = 5 * ee + i
                b = s // 8
                inner = lax.rem(s, 8) * 16
                at = i * 16
                for k in range(5):
                    xperm[pl.ds(al(k * 80 + at, 16), 16), :] = tk_t[
                        pl.ds(al((5 * b + k) * 128 + inner, 16), 16), :
                    ]
                for m in (0, 1):

                    def scale_of(k):
                        return sgu_scales[5 * b + k, pl.ds(m, 1), :]

                    def store(k, value):
                        rows = pl.ds(al(k * 80 + at, 16), 16)
                        wshard[rows, m * HID : (m + 1) * HID] = value

                    digits(gu_all[m, pl.ds(al(s * 16, 16), 16), :], scale_of, store)
                return 0

            lax.fori_loop(0, 5, strip, 0)
            acc_s[...] += jnp.dot(xperm[...].T, wshard[...], preferred_element_type=F32)
            return 0

        lax.fori_loop(0, len(shards_in), one, 0)

    def activate(acc, target):
        g = acc[:, 0:HID]
        h = g / (1.0 + jnp.exp(-g)) * acc[:, HID : 2 * HID]
        target[...] = h.astype(BF16)

    def unpack_down(words, rows_of_scales, target):
        def strip(q, _):
            at = pl.ds(al(q * 16, 16), 16)

            def store(k, value):
                target[pl.ds(al(k * 128 + q * 16, 16), 16), :] = value

            digits(words(at), rows_of_scales, store)
            return 0

        lax.fori_loop(0, 8, strip, 0)

    def routed_chunks(chunks):
        def one(j, _):
            cols = pl.ds(al(HID * pick(j, chunks), 128), HID)
            unpack_down(lambda at: rdn[at, cols], lambda k: dn_scales[k, :, cols], wchunk)
            y = jnp.dot(hid_r[...], wchunk[...], preferred_element_type=F32)
            part_r[cols, :] = y.astype(BF16).T
            return 0

        lax.fori_loop(0, len(chunks), one, 0)

    def shared_down(blocks):
        def one(j, _):
            ee = pick(j, blocks)
            rows = pl.ds(al(BLK * ee, 16), BLK)
            turned[...] = dn_all[rows, :].T
            unpack_down(
                lambda at: turned[at, :], lambda k: scale_blocks[ee, pl.ds(k, 1), :], wblock
            )
            y = jnp.dot(hid_s[...], wblock[...], preferred_element_type=F32)
            part_s[rows, :] = y.astype(BF16).T

            @pl.when(ee // NZ == other)
            def _():
                d = lax.rem(ee, NZ)
                sum_s.sibling_copy(BLK * d, BLK, d).start()

            return 0

        lax.fori_loop(0, len(blocks), one, 0)

    local_tok.wait()
    local_ids.wait()
    expert_row = ids[...]
    onehot = (lax.broadcasted_iota(I32, (16, TOK), 0) == expert_row).astype(F32)
    upto = (
        lax.broadcasted_iota(I32, (TOK, TOK), 0) <= lax.broadcasted_iota(I32, (TOK, TOK), 1)
    ).astype(BF16)
    counted = jnp.dot(onehot.astype(BF16), upto, preferred_element_type=F32)
    rank = jnp.sum(counted * onehot, axis=0, keepdims=True) - 1.0
    slot = expert_row.astype(F32) * 16.0 + rank
    chosen = lax.broadcasted_iota(I32, (SLOTS, TOK), 0).astype(F32) == slot
    select[...] = chosen.astype(F32).astype(BF16)
    disp[...] = lax.dot_general(
        select[...], tk_t[own_rows, :], (((1,), (1,)), ((), ())), preferred_element_type=F32
    ).astype(BF16)
    local_sgu.wait()
    local_sdn.wait()
    local_gs.wait()

    def a2a(src, dst, k):
        def one(i, _):
            to = lax.rem(exp + i, 16)
            copy(
                src.at[pl.ds(al(16 * to, 16), 16), :],
                dst.at[pl.ds(al(16 * exp, 16), 16), :],
                asend.at[k],
                arecv.at[k],
                {"expert": to},
            ).start()
            return 0

        lax.fori_loop(1, 16, one, 0)
        mine = pl.ds(al(16 * exp, 16), 16)
        dst[mine, :] = src[mine, :]

    def a2a_wait(dst, k):
        ref = dst.at[pl.ds(0, 240), :]
        copy(ref, ref, asend.at[k], arecv.at[k], {"seq": other}).wait_recv()

    def a2a_end(src, k):
        ref = src.at[pl.ds(0, 240), :]
        copy(ref, ref, asend.at[k], arecv.at[k], {"seq": other}).wait_send()

    acc_r[...] = jnp.zeros(acc_r.shape, F32)
    acc_s[...] = jnp.zeros(acc_s.shape, F32)
    unpack_routed(0)
    unpack_routed(1)
    pl.semaphore_wait(barrier, 18)

    a2a(disp, disp_in, 0)
    toks.start(True)
    gate.r0()
    up.r0()
    unpack_routed(2)
    toks.start(False)
    unpack_routed(3)
    unpack_routed(4)
    toks.step(1, True)
    unpack_routed(5)
    toks.step(1, False)
    unpack_routed(6)
    toks.step(2, True)
    a2a_wait(disp_in, 0)
    xs_t[own_rows, :] = disp_in[...].T
    slots.start(True)
    toks.step(2, False)
    unpack_routed(7)
    unpack_routed(8)
    toks.step(3, True)
    slots.start(False)
    unpack_routed(9)
    toks.step(3, False)
    toks.step(4, True)
    local_ss.wait()
    local_sds.wait()
    for i in range(16):
        scale_blocks[i, 0:5, :] = sdn_scales[:, BLK * i : BLK * (i + 1)]
    gate.r1()
    up.r1()
    down_a.r0()
    down_b.r0()
    slots.step(1, True)
    for dz in (0, 1, -1, 2, -2, 3, -3, 4):
        toks.sibling_wait(dz)
    shared_shards(gate.arrived(0))
    slots.sibling_wait(0)
    routed_blocks([block_of(core, 0), block_of(other, 0)])
    slots.step(1, False)
    routed_blocks([block_of(core, 1), block_of(core, -1)])
    shared_shards(gate.arrived(1)[0:1])
    slots.step(2, True)
    slots.sibling_wait(1)
    slots.sibling_wait(-1)
    routed_blocks([block_of(other, 1), block_of(other, -1)])
    shared_shards(gate.arrived(1)[1:2])
    slots.step(2, False)
    routed_blocks([block_of(core, 2), block_of(core, -2)])
    shared_shards(gate.arrived(1)[2:3])
    slots.step(3, True)
    slots.sibling_wait(2)
    slots.sibling_wait(-2)
    routed_blocks([block_of(other, 2), block_of(other, -2)])
    shared_shards(gate.arrived(1)[3:4])
    slots.step(3, False)
    routed_blocks([block_of(core, 3), block_of(core, -3)])
    gate.r2()
    up.r2()
    slots.step(4, True)
    down_a.r1()
    down_b.r1()
    slots.sibling_wait(3)
    slots.sibling_wait(-3)
    slots.sibling_wait(4)
    routed_blocks([block_of(c, dz) for c, dz in ((other, 3), (other, -3), (core, 4), (other, 4))])
    activate(acc_r, hid_r)

    local_ds.wait()
    local_dn.wait()
    first = BLK * lax.rem(z + 4, NZ) // HID

    def routed_down(offsets):
        qs = [lax.rem(first + q, 5) for q in offsets]
        routed_chunks([5 * other + q for q in qs])
        for q in qs:
            cp = sum_r.sibling_copy(HID * q, HID, q)
            cp.start()
            sent.append(cp)
        routed_chunks([5 * core + q for q in qs])
        for q in qs:
            sum_r.sibling_wait(HID * q, HID, q)

    routed_down((0, 1))
    sum_r.long_step(0)
    routed_down((4, 2))
    sum_r.short_step(1)
    gate.r3()
    up.r3()
    sum_r.long_step(1)
    down_a.r2()
    down_b.r2()
    routed_down((3,))
    sum_r.short_step(2)
    shared_shards(gate.arrived(2)[0:3])
    sum_r.long_step(2)
    gate.r4()
    up.r4()
    shared_shards(gate.arrived(2)[3:6])
    sum_r.short_step(3)
    down_a.r3()
    down_b.r3()
    shared_shards(gate.arrived(3)[0:2])
    sum_r.long_step(3)
    shared_shards(gate.arrived(3)[2:4])
    shared_shards(gate.arrived(4))
    activate(acc_s, hid_s)
    shared_down(gate.arrived(0))
    back[...] = sum_r.end().astype(BF16).T
    a2a(back, back_in, 1)
    shared_down(gate.arrived(1))
    shared_down(gate.arrived(2))
    shared_down(gate.arrived(3))
    down_a.r4()
    down_b.r4()
    shared_down(gate.arrived(4))

    def shared_wait(offsets):
        for dz in offsets:
            d = lax.rem(z + dz + NZ, NZ)
            sum_s.sibling_wait(BLK * d, BLK, d)

    shared_wait((4,))
    sum_s.long_step(0)
    shared_wait((3, -3))
    sum_s.short_step(1)
    sum_s.long_step(1)
    shared_wait((2, -2))
    sum_s.short_step(2)
    sum_s.long_step(2)
    shared_wait((1, -1))
    sum_s.short_step(3)
    sum_s.long_step(3)
    shared_wait((0,))
    a2a_wait(back_in, 1)
    local_gate.wait()
    routed = lax.dot_general(
        back_in[...], select[...], (((0,), (0,)), ((), ())), preferred_element_type=F32
    )
    out[...] = (sum_s.end() + gate_w[...] * routed).astype(BF16)

    for d in range(NZ):
        sum_s.sibling_copy(BLK * d, BLK, d).wait_send()
    a2a_end(disp, 0)
    a2a_end(back, 1)
    for cp in sent:
        cp.wait_send()


def shards(
    tokens,
    expert_ids,
    gate_weights,
    gate_up_codes,
    gate_up_scales,
    down_codes,
    down_scales,
    shared_gate_up_codes,
    shared_gate_up_scales,
    shared_down_codes,
    shared_down_scales,
):
    hbm = pl.BlockSpec(memory_space=pl.ANY)
    V = pltpu.VMEM
    S = pltpu.SemaphoreType.DMA
    return pl.pallas_call(
        kernel,
        out_shape=jax.ShapeDtypeStruct((BLK, TOK), BF16),
        in_specs=[hbm] * 11,
        out_specs=pl.BlockSpec(memory_space=pltpu.VMEM),
        scratch_shapes=[
            V((1, TOK), I32),
            V((1, TOK), F32),
            V((50, 2, HID), F32),
            V((5, 1, D), F32),
            V((50, 2, HID), F32),
            V((5, D), F32),
            V((16, 8, BLK), F32),
            V((2, 1280, HID), F32),
            V((128, D), F32),
            V((2, 1280, HID), F32),
            V((D, 128), F32),
            V((D, 2 * HID), BF16),
            V((BLK, 2 * HID), BF16),
            V((HID, HID), BF16),
            V((HID, BLK), BF16),
            V((128, BLK), F32),
            V((D, SLOTS), BF16),
            V((D, TOK), BF16),
            V((BLK, TOK), BF16),
            V((SLOTS, 2 * HID), F32),
            V((TOK, 2 * HID), F32),
            V((SLOTS, HID), BF16),
            V((TOK, HID), BF16),
            V((D, SLOTS), BF16),
            V((D, TOK), BF16),
            V((3200, SLOTS), BF16),
            V((3200, TOK), BF16),
            V((4, BLK, SLOTS), BF16),
            V((4, BLK, SLOTS), BF16),
            V((4, BLK, TOK), BF16),
            V((4, BLK, TOK), BF16),
            V((SLOTS, TOK), BF16),
            V((SLOTS, BLK), BF16),
            V((SLOTS, BLK), BF16),
            V((SLOTS, BLK), BF16),
            V((SLOTS, BLK), BF16),
            S((80,)),
            S((80,)),
            S((64,)),
            S((64,)),
            S((2,)),
            S((2,)),
            S((48,)),
            S((48,)),
            S((20,)),
        ],
        compiler_params=pltpu.CompilerParams(
            collective_id=0, has_side_effects=True, vmem_limit_bytes=64 * 1024 * 1024 - 65536
        ),
    )(
        tokens.T,
        expert_ids.reshape(1, TOK),
        gate_weights.reshape(1, TOK),
        gate_up_codes[0],
        jnp.transpose(gate_up_scales[0], (1, 0, 2)),
        down_codes[0],
        jnp.transpose(down_scales, (1, 0, 2)),
        shared_gate_up_codes,
        jnp.transpose(shared_gate_up_scales, (1, 0, 2)),
        shared_down_codes.T,
        shared_down_scales,
    ).T


def solution(mesh):
    placed = (
        P("expert", ("seq", "tensor")),
        P("expert"),
        P("expert"),
        P("expert", None, None, ("seq", "tensor")),
        P("expert", None, None, ("seq", "tensor")),
        P("expert", ("seq", "tensor"), None),
        P("expert", ("seq", "tensor"), None),
        P(None, "expert", ("seq", "tensor")),
        P(None, None, ("seq", "tensor")),
        P(("seq", "tensor"), "expert"),
        P(("seq", "tensor"), None),
    )
    return jax.shard_map(
        shards,
        mesh=mesh,
        in_specs=placed,
        out_specs=P("expert", ("seq", "tensor")),
        check_vma=False,
    )
```

```python
import jax
import jax.numpy as jnp
from jax import lax
from jax.experimental import pallas as pl
from jax.experimental.pallas import tpu as pltpu
from jax.sharding import PartitionSpec as P

MESH = pl.DeviceIdType.MESH
F32 = jnp.float32
BF16 = jnp.bfloat16
I32 = jnp.int32

D = 6400
HID = 640
SLOTS = 256
TOK = 128
BLK = 400
PARTS = ((0, 208), (208, 192), (0, 400))
NZ = 8


def al(value, multiple):
    return pl.multiple_of(value, multiple)


def pick(j, values):
    chosen = values[0]
    for k in range(1, len(values)):
        chosen = lax.select(j == k, values[k], chosen)
    return chosen


def kernel(
    tokens,
    ids_in,
    gate_in,
    gu_codes,
    gu_scales_in,
    dn_codes,
    dn_scales_in,
    sgu_codes,
    sgu_scales_in,
    sdn_codes,
    sdn_scales_in,
    out,
    ids,
    gate_w,
    gu_scales,
    dn_scales,
    sgu_scales,
    sdn_scales,
    scale_blocks,
    rgu,
    rdn,
    gu_all,
    dn_all,
    weights,
    wshard,
    wchunk,
    wblock,
    turned,
    xs_t,
    tk_t,
    xperm,
    acc_r,
    acc_s,
    hid_r,
    hid_s,
    part_r,
    part_s,
    sib_r,
    sib_s,
    precv_r,
    mrecv_r,
    precv_s,
    mrecv_s,
    select,
    disp,
    disp_in,
    back,
    back_in,
    wsend,
    wrecv,
    zsend,
    zrecv,
    asend,
    arecv,
    rsend,
    rrecv,
    lsem,
):
    core = lax.axis_index("seq")
    exp = lax.axis_index("expert")
    z = lax.axis_index("tensor")
    ex = exp // 4
    ey = lax.rem(exp, 4)
    other = 1 - core
    zplus = lax.rem(z + 1, NZ)
    zminus = lax.rem(z + NZ - 1, NZ)

    barrier = pltpu.get_barrier_semaphore()

    def greet(k, _):
        pl.semaphore_signal(
            barrier, inc=1, device_id={"expert": lax.rem(exp + k, 16)}, device_id_type=MESH
        )
        return 0

    pl.semaphore_signal(barrier, inc=1, device_id={"seq": other}, device_id_type=MESH)
    pl.semaphore_signal(barrier, inc=1, device_id={"tensor": zplus}, device_id_type=MESH)
    pl.semaphore_signal(barrier, inc=1, device_id={"tensor": zminus}, device_id_type=MESH)
    lax.fori_loop(1, 16, greet, 0)

    def load(src, dst, k):
        cp = pltpu.make_async_copy(src, dst, lsem.at[k])
        cp.start()
        return cp

    own_rows = pl.ds(al(3200 * core + BLK * z, 16), BLK)
    dn_rows = pl.ds(al(BLK * exp, 16), BLK)
    local_tok = load(tokens, tk_t.at[own_rows, :], 0)
    local_ids = load(ids_in, ids, 1)
    local_gate = load(gate_in, gate_w, 2)
    local_sgu = load(sgu_codes, gu_all.at[:, pl.ds(al(80 * exp, 8), 80), :], 3)
    local_sdn = load(sdn_codes, dn_all.at[dn_rows, :], 4)
    local_gs = load(gu_scales_in, gu_scales, 5)
    local_gu = []
    for b in range(10):
        rows = pl.ds(128 * b, 128)
        local_gu.append(load(gu_codes.at[:, rows, :], rgu.at[:, rows, :], 10 + b))
    local_dn = load(dn_codes, rdn, 6)
    local_ds = load(dn_scales_in, dn_scales, 7)
    local_ss = load(sgu_scales_in, sgu_scales, 8)
    local_sds = load(sdn_scales_in, sdn_scales, 9)

    sent = []

    def copy(src, dst, ssem, rsem, device):
        return pltpu.make_async_remote_copy(
            src_ref=src,
            dst_ref=dst,
            send_sem=ssem,
            recv_sem=rsem,
            device_id=device,
            device_id_type=MESH,
        )

    def push(src, dst, ssem, rsem, device):
        cp = copy(src, dst, ssem, rsem, device)
        cp.start()
        sent.append(cp)

    def region(piece, ee, half):
        if piece < 2:
            off, size = ((0, 80), (0, 40), (40, 40))[half]
            return gu_all.at[piece, pl.ds(al(80 * ee + off, 8), size), :]
        base = 200 * (piece - 2)
        off, size = ((0, 200), (0, 104), (104, 96))[half]
        return dn_all.at[pl.ds(al(400 * ee + (base + off), 8), size), :]

    class Piece:
        def __init__(self, piece):
            self.piece = piece
            self.by_x = piece % 2 == 0
            self.a = ex if self.by_x else ey
            self.b = ey if self.by_x else ex

        def block(self, da, db):
            a = lax.rem(self.a + da + 4, 4)
            b = lax.rem(self.b + db + 4, 4)
            return a * 4 + b if self.by_x else b * 4 + a

        def send(self, sem, da, db, half, step_a, step_b):
            ref = region(self.piece, self.block(da, db), half)
            s = 20 * self.piece + sem
            push(ref, ref, wsend.at[s], wrecv.at[s], {"expert": self.block(step_a, step_b)})

        def wait(self, sem, da, db, half):
            ref = region(self.piece, self.block(da, db), half)
            s = 20 * self.piece + sem
            copy(ref, ref, wsend.at[s], wrecv.at[s], {"expert": self.block(1, 0)}).wait_recv()

        def stage2(self, q, da):
            self.send(4 + 4 * q, da, 0, 0, 0, 1)
            self.send(5 + 4 * q, da, 0, 0, 0, -1)

        def stage2_forward(self, q, da):
            self.wait(4 + 4 * q, da, -1, 0)
            self.send(6 + 4 * q, da, -1, 1, 0, 1)
            self.wait(5 + 4 * q, da, 1, 0)
            self.send(7 + 4 * q, da, 1, 2, 0, -1)

        def stage2_end(self, q, da):
            self.wait(6 + 4 * q, da, 2, 1)
            self.wait(7 + 4 * q, da, 2, 2)

        def r0(self):
            self.send(0, 0, 0, 0, 1, 0)
            self.send(1, 0, 0, 0, -1, 0)
            self.stage2(0, 0)

        def r1(self):
            self.wait(0, -1, 0, 0)
            self.send(2, -1, 0, 1, 1, 0)
            self.stage2(1, -1)
            self.wait(1, 1, 0, 0)
            self.send(3, 1, 0, 2, -1, 0)
            self.stage2(2, 1)
            self.stage2_forward(0, 0)

        def r2(self):
            self.wait(2, 2, 0, 1)
            self.wait(3, 2, 0, 2)
            self.stage2(3, 2)
            self.stage2_forward(1, -1)
            self.stage2_forward(2, 1)
            self.stage2_end(0, 0)

        def r3(self):
            self.stage2_forward(3, 2)
            self.stage2_end(1, -1)
            self.stage2_end(2, 1)

        def r4(self):
            self.stage2_end(3, 2)

        def arrived(self, r):
            places = (
                ((0, 0),),
                ((-1, 0), (1, 0), (0, -1), (0, 1)),
                ((2, 0), (0, 2), (-1, -1), (-1, 1), (1, -1), (1, 1)),
                ((2, -1), (2, 1), (-1, 2), (1, 2)),
                ((2, 2),),
            )[r]
            return [self.block(da, db) for da, db in places]

    gate, up, down_a, down_b = (Piece(i) for i in range(4))

    def block_of(c, dz):
        return NZ * c + lax.rem(z + dz + NZ, NZ)

    class Gather:
        def __init__(self, ref, which):
            self.ref = ref
            self.base = 32 * which

        def rows(self, c, dz, part):
            off, size = PARTS[part]
            return self.ref.at[pl.ds(al(BLK * block_of(c, dz) + off, 16), size), :]

        def ring(self, up_way, r, part):
            ref = self.rows(core, -r if up_way else r, part)
            k = self.base + (0 if up_way else 8) + 2 * r + part
            to = zplus if up_way else zminus
            push(ref, ref, zsend.at[k], zrecv.at[k], {"tensor": to})

        def sibling(self, dz, part):
            ref = self.rows(core, dz, part)
            k = self.base + 16 + 2 * (dz % NZ) + part
            push(ref, ref, zsend.at[k], zrecv.at[k], {"seq": other})

        def ring_wait(self, up_way, r, part):
            ref = self.rows(core, -r if up_way else r, part)
            k = self.base + (0 if up_way else 8) + 2 * (r - 1) + part
            copy(ref, ref, zsend.at[k], zrecv.at[k], {"tensor": zplus}).wait_recv()

        def sibling_wait(self, dz):
            for part in (0, 1):
                ref = self.rows(other, dz, part)
                k = self.base + 16 + 2 * (dz % NZ) + part
                copy(ref, ref, zsend.at[k], zrecv.at[k], {"seq": other}).wait_recv()

        def start(self, long_way):
            part = 0 if long_way else 1
            self.ring(True, 0, part)
            self.ring(False, 0, 1 - part)
            self.sibling(0, part)

        def step(self, r, long_way):
            for up_way in (True, False):
                part = 0 if long_way == up_way else 1
                self.ring_wait(up_way, r, part)
                if r <= (3 if long_way else 2):
                    self.ring(up_way, r, part)
                self.sibling(-r if up_way else r, part)

    slots = Gather(xs_t, 0)
    toks = Gather(tk_t, 1)

    class Scatter:
        def __init__(self, which, part, sib, precv, mrecv):
            self.base = 24 * which
            self.part, self.sib = part, sib
            self.recv = (precv, mrecv)

        def sibling_copy(self, at, size, k):
            return copy(
                self.part.at[pl.ds(al(3200 * other + at, 16), size), :],
                self.sib.at[pl.ds(al(at, 16), size), :],
                rsend.at[self.base + k],
                rrecv.at[self.base + k],
                {"seq": other},
            )

        def sibling_wait(self, at, size, k):
            ref = self.sib.at[pl.ds(al(at, 16), size), :]
            k = self.base + k
            copy(ref, ref, rsend.at[k], rrecv.at[k], {"seq": other}).wait_recv()

        def pair(self, d, part):
            lo, size = PARTS[part]
            mine = self.part[pl.ds(al(BLK * (NZ * core + d) + lo, 16), size), :]
            theirs = self.sib[pl.ds(al(BLK * d + lo, 16), size), :]
            return mine.astype(F32) + theirs.astype(F32)

        def slot(self, way, s, part):
            lo, size = PARTS[part]
            return self.recv[way].at[s, pl.ds(lo, size), :]

        def wait(self, way, s, part):
            ref = self.slot(way, s, part)
            k = self.base + 8 + 8 * way + 2 * s + part
            copy(ref, ref, rsend.at[k], rrecv.at[k], {"tensor": zplus}).wait_recv()

        def message(self, way, s, part):
            lo, size = PARTS[part]
            d = lax.rem(z + (4 - s if way == 0 else s - 4) + NZ, NZ)
            value = self.pair(d, part)
            if s > (0 if way == part else 1):
                self.wait(way, s - 1, part)
                value = value + self.recv[way][s - 1, pl.ds(lo, size), :].astype(F32)
            rows = pl.ds(al(BLK * (NZ * core + d) + lo, 16), size)
            self.part[rows, :] = value.astype(BF16)
            k = self.base + 8 + 8 * way + 2 * s + part
            push(
                self.part.at[rows, :],
                self.slot(way, s, part),
                rsend.at[k],
                rrecv.at[k],
                {"tensor": zplus if way == 0 else zminus},
            )

        def long_step(self, s):
            self.message(0, s, 0)
            self.message(1, s, 1)

        def short_step(self, s):
            self.message(0, s, 1)
            self.message(1, s, 0)

        def end(self):
            for way in (0, 1):
                for part in (0, 1):
                    self.wait(way, 3, part)
            return (
                self.pair(z, 2)
                + self.recv[0][3].astype(F32)
                + self.recv[1][3].astype(F32)
            )

    sum_r = Scatter(0, part_r, sib_r, precv_r, mrecv_r)
    sum_s = Scatter(1, part_s, sib_s, precv_s, mrecv_s)

    def digits(words, scale_of, store):
        w = words.astype(I32) ^ 0x88888
        for k in range(5):
            code = lax.shift_right_arithmetic(lax.shift_left(w, I32(28 - 4 * k)), I32(28))
            store(k, (code.astype(F32) * scale_of(k)).astype(BF16))

    def unpack_routed(b):
        local_gu[b].wait()

        def one(i, _):
            inner = i * 16
            for m in (0, 1):

                def scale_of(k):
                    return gu_scales[5 * b + k, pl.ds(m, 1), :]

                def store(k, value):
                    rows = pl.ds(al((5 * b + k) * 128 + inner, 16), 16)
                    weights[rows, m * HID : (m + 1) * HID] = value

                digits(rgu[m, pl.ds(al(128 * b + inner, 16), 16), :], scale_of, store)
            return 0

        lax.fori_loop(0, 8, one, 0)

    def routed_blocks(blocks):
        def one(j, _):
            rows = pl.ds(al(BLK * pick(j, blocks), 16), BLK)
            acc_r[...] += jnp.dot(
                xs_t[rows, :].T, weights[rows, :], preferred_element_type=F32
            )
            return 0

        lax.fori_loop(0, len(blocks), one, 0)

    def shared_shards(shards_in):
        def one(j, _):
            ee = pick(j, shards_in)

            def strip(i, _):
                s = 5 * ee + i
                b = s // 8
                inner = lax.rem(s, 8) * 16
                at = i * 16
                for k in range(5):
                    xperm[pl.ds(al(k * 80 + at, 16), 16), :] = tk_t[
                        pl.ds(al((5 * b + k) * 128 + inner, 16), 16), :
                    ]
                for m in (0, 1):

                    def scale_of(k):
                        return sgu_scales[5 * b + k, pl.ds(m, 1), :]

                    def store(k, value):
                        rows = pl.ds(al(k * 80 + at, 16), 16)
                        wshard[rows, m * HID : (m + 1) * HID] = value

                    digits(gu_all[m, pl.ds(al(s * 16, 16), 16), :], scale_of, store)
                return 0

            lax.fori_loop(0, 5, strip, 0)
            acc_s[...] += jnp.dot(xperm[...].T, wshard[...], preferred_element_type=F32)
            return 0

        lax.fori_loop(0, len(shards_in), one, 0)

    def activate(acc, target):
        g = acc[:, 0:HID]
        h = g / (1.0 + jnp.exp(-g)) * acc[:, HID : 2 * HID]
        target[...] = h.astype(BF16)

    def unpack_down(words, rows_of_scales, target):
        def strip(q, _):
            at = pl.ds(al(q * 16, 16), 16)

            def store(k, value):
                target[pl.ds(al(k * 128 + q * 16, 16), 16), :] = value

            digits(words(at), rows_of_scales, store)
            return 0

        lax.fori_loop(0, 8, strip, 0)

    def routed_chunks(chunks):
        def one(j, _):
            cols = pl.ds(al(HID * pick(j, chunks), 128), HID)
            unpack_down(lambda at: rdn[at, cols], lambda k: dn_scales[k, :, cols], wchunk)
            y = jnp.dot(hid_r[...], wchunk[...], preferred_element_type=F32)
            part_r[cols, :] = y.astype(BF16).T
            return 0

        lax.fori_loop(0, len(chunks), one, 0)

    def shared_down(blocks):
        def one(j, _):
            ee = pick(j, blocks)
            rows = pl.ds(al(BLK * ee, 16), BLK)
            turned[...] = dn_all[rows, :].T
            unpack_down(
                lambda at: turned[at, :], lambda k: scale_blocks[ee, pl.ds(k, 1), :], wblock
            )
            y = jnp.dot(hid_s[...], wblock[...], preferred_element_type=F32)
            part_s[rows, :] = y.astype(BF16).T
            return 0

        lax.fori_loop(0, len(blocks), one, 0)

    local_tok.wait()
    local_ids.wait()
    expert_row = ids[...]
    onehot = (lax.broadcasted_iota(I32, (16, TOK), 0) == expert_row).astype(F32)
    upto = (
        lax.broadcasted_iota(I32, (TOK, TOK), 0) <= lax.broadcasted_iota(I32, (TOK, TOK), 1)
    ).astype(BF16)
    counted = jnp.dot(onehot.astype(BF16), upto, preferred_element_type=F32)
    rank = jnp.sum(counted * onehot, axis=0, keepdims=True) - 1.0
    slot = expert_row.astype(F32) * 16.0 + rank
    chosen = lax.broadcasted_iota(I32, (SLOTS, TOK), 0).astype(F32) == slot
    select[...] = chosen.astype(F32).astype(BF16)
    disp[...] = lax.dot_general(
        select[...], tk_t[own_rows, :], (((1,), (1,)), ((), ())), preferred_element_type=F32
    ).astype(BF16)
    local_sgu.wait()
    local_sdn.wait()
    local_gs.wait()

    def a2a(src, dst, k):
        def one(i, _):
            to = lax.rem(exp + i, 16)
            copy(
                src.at[pl.ds(al(16 * to, 16), 16), :],
                dst.at[pl.ds(al(16 * exp, 16), 16), :],
                asend.at[k],
                arecv.at[k],
                {"expert": to},
            ).start()
            return 0

        lax.fori_loop(1, 16, one, 0)
        mine = pl.ds(al(16 * exp, 16), 16)
        dst[mine, :] = src[mine, :]

    def a2a_wait(dst, k):
        ref = dst.at[pl.ds(0, 240), :]
        copy(ref, ref, asend.at[k], arecv.at[k], {"seq": other}).wait_recv()

    def a2a_end(src, k):
        ref = src.at[pl.ds(0, 240), :]
        copy(ref, ref, asend.at[k], arecv.at[k], {"seq": other}).wait_send()

    acc_r[...] = jnp.zeros(acc_r.shape, F32)
    acc_s[...] = jnp.zeros(acc_s.shape, F32)
    unpack_routed(0)
    unpack_routed(1)
    pl.semaphore_wait(barrier, 18)

    a2a(disp, disp_in, 0)
    toks.start(True)
    gate.r0()
    up.r0()
    unpack_routed(2)
    toks.start(False)
    unpack_routed(3)
    down_a.r0()
    down_b.r0()
    unpack_routed(4)
    toks.step(1, True)
    unpack_routed(5)
    toks.step(1, False)
    unpack_routed(6)
    a2a_wait(disp_in, 0)
    xs_t[own_rows, :] = disp_in[...].T
    slots.start(True)
    toks.step(2, True)
    unpack_routed(7)
    toks.step(2, False)
    unpack_routed(8)
    slots.start(False)
    unpack_routed(9)
    toks.step(3, True)
    local_ss.wait()
    local_sds.wait()
    for i in range(16):
        scale_blocks[i, 0:5, :] = sdn_scales[:, BLK * i : BLK * (i + 1)]
    down_a.r1()
    down_b.r1()
    toks.step(3, False)
    gate.r1()
    up.r1()
    slots.step(1, True)
    toks.step(4, True)
    slots.sibling_wait(0)
    routed_blocks([block_of(core, 0), block_of(other, 0)])
    slots.step(1, False)
    routed_blocks([block_of(core, 1), block_of(core, -1)])
    for dz in (0, 1, -1, 2, -2, 3, -3, 4):
        toks.sibling_wait(dz)
    shared_shards(gate.arrived(0))
    slots.step(2, True)
    slots.sibling_wait(1)
    slots.sibling_wait(-1)
    routed_blocks([block_of(other, 1), block_of(other, -1)])
    shared_shards(gate.arrived(1)[0:1])
    slots.step(2, False)
    routed_blocks([block_of(core, 2), block_of(core, -2)])
    shared_shards(gate.arrived(1)[1:2])
    slots.step(3, True)
    slots.sibling_wait(2)
    slots.sibling_wait(-2)
    routed_blocks([block_of(other, 2), block_of(other, -2)])
    shared_shards(gate.arrived(1)[2:3])
    slots.step(3, False)
    routed_blocks([block_of(core, 3), block_of(core, -3)])
    shared_shards(gate.arrived(1)[3:4])
    down_a.r2()
    down_b.r2()
    slots.step(4, True)
    slots.sibling_wait(3)
    slots.sibling_wait(-3)
    slots.sibling_wait(4)
    routed_blocks([block_of(c, dz) for c, dz in ((other, 3), (other, -3), (core, 4), (other, 4))])
    activate(acc_r, hid_r)

    local_ds.wait()
    local_dn.wait()
    first = BLK * lax.rem(z + 4, NZ) // HID

    def routed_down(offsets):
        qs = [lax.rem(first + q, 5) for q in offsets]
        routed_chunks([5 * other + q for q in qs])
        for q in qs:
            cp = sum_r.sibling_copy(HID * q, HID, q)
            cp.start()
            sent.append(cp)
        routed_chunks([5 * core + q for q in qs])
        for q in qs:
            sum_r.sibling_wait(HID * q, HID, q)

    routed_down((0, 1))
    sum_r.long_step(0)
    gate.r2()
    up.r2()
    routed_down((4, 2))
    sum_r.short_step(1)
    sum_r.long_step(1)
    routed_down((3,))
    down_a.r3()
    down_b.r3()
    shared_shards(gate.arrived(2)[0:2])
    sum_r.short_step(2)
    shared_shards(gate.arrived(2)[2:3])
    sum_r.long_step(2)
    shared_shards(gate.arrived(2)[3:6])
    gate.r3()
    up.r3()
    sum_r.short_step(3)
    shared_shards(gate.arrived(3)[0:1])
    sum_r.long_step(3)
    shared_shards(gate.arrived(3)[1:4])
    down_a.r4()
    down_b.r4()
    gate.r4()
    up.r4()
    shared_shards(gate.arrived(4))
    activate(acc_s, hid_s)

    def shared_order(offsets):
        ds = [lax.rem(z + dz + NZ, NZ) for dz in offsets]
        shared_down([NZ * other + d for d in ds])
        for d in ds:
            cp = sum_s.sibling_copy(BLK * d, BLK, d)
            cp.start()
            sent.append(cp)
        shared_down([NZ * core + d for d in ds])
        for d in ds:
            sum_s.sibling_wait(BLK * d, BLK, d)

    shared_order((4,))
    sum_s.long_step(0)
    back[...] = sum_r.end().astype(BF16).T
    a2a(back, back_in, 1)
    shared_order((3, -3))
    sum_s.short_step(1)
    sum_s.long_step(1)
    shared_order((2, -2))
    sum_s.short_step(2)
    sum_s.long_step(2)
    shared_order((1, -1))
    sum_s.short_step(3)
    sum_s.long_step(3)
    shared_order((0,))
    a2a_wait(back_in, 1)
    local_gate.wait()
    routed = lax.dot_general(
        back_in[...], select[...], (((0,), (0,)), ((), ())), preferred_element_type=F32
    )
    out[...] = (sum_s.end() + gate_w[...] * routed).astype(BF16)

    a2a_end(disp, 0)
    a2a_end(back, 1)
    for cp in sent:
        cp.wait_send()


def shards(
    tokens,
    expert_ids,
    gate_weights,
    gate_up_codes,
    gate_up_scales,
    down_codes,
    down_scales,
    shared_gate_up_codes,
    shared_gate_up_scales,
    shared_down_codes,
    shared_down_scales,
):
    hbm = pl.BlockSpec(memory_space=pl.ANY)
    V = pltpu.VMEM
    S = pltpu.SemaphoreType.DMA
    return pl.pallas_call(
        kernel,
        out_shape=jax.ShapeDtypeStruct((BLK, TOK), BF16),
        in_specs=[hbm] * 11,
        out_specs=pl.BlockSpec(memory_space=pltpu.VMEM),
        scratch_shapes=[
            V((1, TOK), I32),
            V((1, TOK), F32),
            V((50, 2, HID), F32),
            V((5, 1, D), F32),
            V((50, 2, HID), F32),
            V((5, D), F32),
            V((16, 8, BLK), F32),
            V((2, 1280, HID), F32),
            V((128, D), F32),
            V((2, 1280, HID), F32),
            V((D, 128), F32),
            V((D, 2 * HID), BF16),
            V((BLK, 2 * HID), BF16),
            V((HID, HID), BF16),
            V((HID, BLK), BF16),
            V((128, BLK), F32),
            V((D, SLOTS), BF16),
            V((D, TOK), BF16),
            V((BLK, TOK), BF16),
            V((SLOTS, 2 * HID), F32),
            V((TOK, 2 * HID), F32),
            V((SLOTS, HID), BF16),
            V((TOK, HID), BF16),
            V((D, SLOTS), BF16),
            V((D, TOK), BF16),
            V((3200, SLOTS), BF16),
            V((3200, TOK), BF16),
            V((4, BLK, SLOTS), BF16),
            V((4, BLK, SLOTS), BF16),
            V((4, BLK, TOK), BF16),
            V((4, BLK, TOK), BF16),
            V((SLOTS, TOK), BF16),
            V((SLOTS, BLK), BF16),
            V((SLOTS, BLK), BF16),
            V((SLOTS, BLK), BF16),
            V((SLOTS, BLK), BF16),
            S((80,)),
            S((80,)),
            S((64,)),
            S((64,)),
            S((2,)),
            S((2,)),
            S((48,)),
            S((48,)),
            S((20,)),
        ],
        compiler_params=pltpu.CompilerParams(
            collective_id=0, has_side_effects=True, vmem_limit_bytes=64 * 1024 * 1024 - 65536
        ),
    )(
        tokens.T,
        expert_ids.reshape(1, TOK),
        gate_weights.reshape(1, TOK),
        gate_up_codes[0],
        jnp.transpose(gate_up_scales[0], (1, 0, 2)),
        down_codes[0],
        jnp.transpose(down_scales, (1, 0, 2)),
        shared_gate_up_codes,
        jnp.transpose(shared_gate_up_scales, (1, 0, 2)),
        shared_down_codes.T,
        shared_down_scales,
    ).T


def solution(mesh):
    placed = (
        P("expert", ("seq", "tensor")),
        P("expert"),
        P("expert"),
        P("expert", None, None, ("seq", "tensor")),
        P("expert", None, None, ("seq", "tensor")),
        P("expert", ("seq", "tensor"), None),
        P("expert", ("seq", "tensor"), None),
        P(None, "expert", ("seq", "tensor")),
        P(None, None, ("seq", "tensor")),
        P(("seq", "tensor"), "expert"),
        P(("seq", "tensor"), None),
    )
    return jax.shard_map(
        shards,
        mesh=mesh,
        in_specs=placed,
        out_specs=P("expert", ("seq", "tensor")),
        check_vma=False,
    )
```

```python
import jax
import jax.numpy as jnp
from jax import lax
from jax.experimental import pallas as pl
from jax.experimental.pallas import tpu as pltpu
from jax.sharding import PartitionSpec as P

MESH = pl.DeviceIdType.MESH
F32 = jnp.float32
BF16 = jnp.bfloat16
I32 = jnp.int32

D = 6400
HID = 640
SLOTS = 256
TOK = 128
BLK = 400
PARTS = ((0, 208), (208, 192), (0, 400))
NZ = 8


def al(value, multiple):
    return pl.multiple_of(value, multiple)


def pick(j, values):
    chosen = values[0]
    for k in range(1, len(values)):
        chosen = lax.select(j == k, values[k], chosen)
    return chosen


def kernel(
    tokens,
    ids_in,
    gate_in,
    gu_codes,
    gu_scales_in,
    dn_codes,
    dn_scales_in,
    sgu_codes,
    sgu_scales_in,
    sdn_codes,
    sdn_scales_in,
    out,
    ids,
    gate_w,
    gu_scales,
    dn_scales,
    sgu_scales,
    sdn_scales,
    rgu,
    rdn,
    own_gu,
    own_dn,
    packed,
    turn_in,
    weights,
    wshard,
    wchunk,
    turned,
    xs_t,
    tk_t,
    xperm,
    acc_r,
    acc_s,
    hid_r,
    hid_s,
    part_r,
    part_s,
    sib_r,
    sib_s,
    precv_r,
    mrecv_r,
    precv_s,
    mrecv_s,
    select,
    disp,
    disp_in,
    back,
    back_in,
    wsend,
    wrecv,
    zsend,
    zrecv,
    asend,
    arecv,
    rsend,
    rrecv,
    lsem,
):
    core = lax.axis_index("seq")
    exp = lax.axis_index("expert")
    z = lax.axis_index("tensor")
    ex = exp // 4
    ey = lax.rem(exp, 4)
    other = 1 - core
    zplus = lax.rem(z + 1, NZ)
    zminus = lax.rem(z + NZ - 1, NZ)

    barrier = pltpu.get_barrier_semaphore()

    def greet(k, _):
        pl.semaphore_signal(
            barrier, inc=1, device_id={"expert": lax.rem(exp + k, 16)}, device_id_type=MESH
        )
        return 0

    pl.semaphore_signal(barrier, inc=1, device_id={"seq": other}, device_id_type=MESH)
    pl.semaphore_signal(barrier, inc=1, device_id={"tensor": zplus}, device_id_type=MESH)
    pl.semaphore_signal(barrier, inc=1, device_id={"tensor": zminus}, device_id_type=MESH)
    lax.fori_loop(1, 16, greet, 0)

    def load(src, dst, k):
        cp = pltpu.make_async_copy(src, dst, lsem.at[k])
        cp.start()
        return cp

    own_rows = pl.ds(al(3200 * core + BLK * z, 16), BLK)
    local_tok = load(tokens, tk_t.at[own_rows, :], 0)
    local_ids = load(ids_in, ids, 1)
    local_gate = load(gate_in, gate_w, 2)
    local_sgu = load(sgu_codes, own_gu, 3)
    local_sdn = load(sdn_codes, own_dn, 4)
    local_gs = load(gu_scales_in, gu_scales, 5)
    local_gu = []
    for b in range(10):
        rows = pl.ds(128 * b, 128)
        local_gu.append(load(gu_codes.at[:, rows, :], rgu.at[:, rows, :], 10 + b))
    local_dn = load(dn_codes, rdn, 6)
    local_ds = load(dn_scales_in, dn_scales, 7)
    local_ss = load(sgu_scales_in, sgu_scales, 8)
    local_sds = load(sdn_scales_in, sdn_scales, 9)

    sent = []

    def copy(src, dst, ssem, rsem, device):
        return pltpu.make_async_remote_copy(
            src_ref=src,
            dst_ref=dst,
            send_sem=ssem,
            recv_sem=rsem,
            device_id=device,
            device_id_type=MESH,
        )

    def push(src, dst, ssem, rsem, device):
        cp = copy(src, dst, ssem, rsem, device)
        cp.start()
        sent.append(cp)

    def drain(keep):
        while len(sent) > keep:
            sent.pop(0).wait_send()

    def pack_own():
        for r in range(10):
            for c in range(5):
                rows, cols = pl.ds(8 * r, 8), pl.ds(128 * c, 128)
                g = own_gu[0, rows, cols].astype(I32)
                u = own_gu[1, rows, cols].astype(I32)
                d = own_dn[pl.ds(8 * (5 * r + c), 8), :].astype(I32)
                low = (g | lax.shift_left(u, I32(20))) ^ I32(-0x77777778)
                high = (lax.shift_right_logical(u, I32(12)) | lax.shift_left(d, I32(8))) ^ I32(0x08888888)
                at = pl.ds(al(80 * exp + 8 * r, 8), 8)
                packed[0, at, cols] = low
                packed[1, at, cols] = high

    def region(piece, ee, half):
        off, size = ((0, 80), (0, 40), (40, 40))[half]
        return packed.at[piece, pl.ds(al(80 * ee + off, 8), size), :]

    class Piece:
        def __init__(self, piece):
            self.piece = piece
            self.by_x = piece % 2 == 0
            self.a = ex if self.by_x else ey
            self.b = ey if self.by_x else ex

        def block(self, da, db):
            a = lax.rem(self.a + da + 4, 4)
            b = lax.rem(self.b + db + 4, 4)
            return a * 4 + b if self.by_x else b * 4 + a

        def send(self, sem, da, db, half, step_a, step_b):
            ref = region(self.piece, self.block(da, db), half)
            s = 20 * self.piece + sem
            push(ref, ref, wsend.at[s], wrecv.at[s], {"expert": self.block(step_a, step_b)})

        def wait(self, sem, da, db, half):
            ref = region(self.piece, self.block(da, db), half)
            s = 20 * self.piece + sem
            copy(ref, ref, wsend.at[s], wrecv.at[s], {"expert": self.block(1, 0)}).wait_recv()

        def stage2(self, q, da):
            self.send(4 + 4 * q, da, 0, 0, 0, 1)
            self.send(5 + 4 * q, da, 0, 0, 0, -1)

        def stage2_forward(self, q, da):
            self.wait(4 + 4 * q, da, -1, 0)
            self.send(6 + 4 * q, da, -1, 1, 0, 1)
            self.wait(5 + 4 * q, da, 1, 0)
            self.send(7 + 4 * q, da, 1, 2, 0, -1)

        def stage2_end(self, q, da):
            self.wait(6 + 4 * q, da, 2, 1)
            self.wait(7 + 4 * q, da, 2, 2)

        def r0(self):
            self.send(0, 0, 0, 0, 1, 0)
            self.send(1, 0, 0, 0, -1, 0)
            self.stage2(0, 0)

        def r1(self):
            self.wait(0, -1, 0, 0)
            self.send(2, -1, 0, 1, 1, 0)
            self.stage2(1, -1)
            self.wait(1, 1, 0, 0)
            self.send(3, 1, 0, 2, -1, 0)
            self.stage2(2, 1)
            self.stage2_forward(0, 0)

        def r2(self):
            self.wait(2, 2, 0, 1)
            self.wait(3, 2, 0, 2)
            self.stage2(3, 2)
            self.stage2_forward(1, -1)
            self.stage2_forward(2, 1)
            self.stage2_end(0, 0)

        def r3(self):
            self.stage2_forward(3, 2)
            self.stage2_end(1, -1)
            self.stage2_end(2, 1)

        def r4(self):
            self.stage2_end(3, 2)

        def arrived(self, r):
            places = (
                ((0, 0),),
                ((-1, 0), (1, 0), (0, -1), (0, 1)),
                ((2, 0), (0, 2), (-1, -1), (-1, 1), (1, -1), (1, 1)),
                ((2, -1), (2, 1), (-1, 2), (1, 2)),
                ((2, 2),),
            )[r]
            return [self.block(da, db) for da, db in places]

    low, high = Piece(0), Piece(1)

    def block_of(c, dz):
        return NZ * c + lax.rem(z + dz + NZ, NZ)

    class Gather:
        def __init__(self, ref, which):
            self.ref = ref
            self.base = 32 * which

        def rows(self, c, dz, part):
            off, size = PARTS[part]
            return self.ref.at[pl.ds(al(BLK * block_of(c, dz) + off, 16), size), :]

        def ring(self, up_way, r, part):
            ref = self.rows(core, -r if up_way else r, part)
            k = self.base + (0 if up_way else 8) + 2 * r + part % 2
            to = zplus if up_way else zminus
            push(ref, ref, zsend.at[k], zrecv.at[k], {"tensor": to})

        def sibling(self, dz):
            ref = self.rows(core, dz, 2)
            k = self.base + 16 + dz % NZ
            push(ref, ref, zsend.at[k], zrecv.at[k], {"seq": other})

        def ring_wait(self, up_way, r, part):
            ref = self.rows(core, -r if up_way else r, part)
            k = self.base + (0 if up_way else 8) + 2 * (r - 1) + part % 2
            copy(ref, ref, zsend.at[k], zrecv.at[k], {"tensor": zplus}).wait_recv()

        def sibling_wait(self, dz):
            ref = self.rows(other, dz, 2)
            k = self.base + 16 + dz % NZ
            copy(ref, ref, zsend.at[k], zrecv.at[k], {"seq": other}).wait_recv()

        def start(self, long_way):
            part = 0 if long_way else 1
            self.ring(True, 0, part)
            self.ring(False, 0, 1 - part)
            if long_way:
                self.sibling(0)

        def step(self, r, long_way):
            for up_way in (True, False):
                part = 0 if long_way == up_way else 1
                self.ring_wait(up_way, r, part)
                if r <= (3 if long_way else 2):
                    self.ring(up_way, r, part)
                if not long_way:
                    self.sibling(-r if up_way else r)
            if r == 4:
                self.sibling(4)

        def start_whole(self):
            self.ring(True, 0, 2)
            self.ring(False, 0, 2)
            self.sibling(0)

        def step_whole(self, r):
            self.ring_wait(True, r, 2)
            if r <= 3:
                self.ring(True, r, 2)
            self.sibling(-r)
            if r <= 3:
                self.ring_wait(False, r, 2)
                if r <= 2:
                    self.ring(False, r, 2)
                self.sibling(r)

    slots = Gather(xs_t, 0)
    toks = Gather(tk_t, 1)

    class Scatter:
        def __init__(self, which, part, sib, precv, mrecv):
            self.base = 24 * which
            self.part, self.sib = part, sib
            self.recv = (precv, mrecv)

        def sibling_copy(self, at, size, k):
            return copy(
                self.part.at[pl.ds(al(3200 * other + at, 16), size), :],
                self.sib.at[pl.ds(al(at, 16), size), :],
                rsend.at[self.base + k],
                rrecv.at[self.base + k],
                {"seq": other},
            )

        def sibling_wait(self, at, size, k):
            ref = self.sib.at[pl.ds(al(at, 16), size), :]
            k = self.base + k
            copy(ref, ref, rsend.at[k], rrecv.at[k], {"seq": other}).wait_recv()

        def pair(self, d, part):
            lo, size = PARTS[part]
            mine = self.part[pl.ds(al(BLK * (NZ * core + d) + lo, 16), size), :]
            theirs = self.sib[pl.ds(al(BLK * d + lo, 16), size), :]
            return mine.astype(F32) + theirs.astype(F32)

        def slot(self, way, s, part):
            lo, size = PARTS[part]
            return self.recv[way].at[s, pl.ds(lo, size), :]

        def wait(self, way, s, part):
            ref = self.slot(way, s, part)
            k = self.base + 8 + 8 * way + 2 * s + part
            copy(ref, ref, rsend.at[k], rrecv.at[k], {"tensor": zplus}).wait_recv()

        def message(self, way, s, part):
            lo, size = PARTS[part]
            d = lax.rem(z + (4 - s if way == 0 else s - 4) + NZ, NZ)
            value = self.pair(d, part)
            if s > (0 if way == part else 1):
                self.wait(way, s - 1, part)
                value = value + self.recv[way][s - 1, pl.ds(lo, size), :].astype(F32)
            rows = pl.ds(al(BLK * (NZ * core + d) + lo, 16), size)
            self.part[rows, :] = value.astype(BF16)
            k = self.base + 8 + 8 * way + 2 * s + part
            push(
                self.part.at[rows, :],
                self.slot(way, s, part),
                rsend.at[k],
                rrecv.at[k],
                {"tensor": zplus if way == 0 else zminus},
            )

        def long_step(self, s):
            self.message(0, s, 0)
            self.message(1, s, 1)

        def short_step(self, s):
            self.message(0, s, 1)
            self.message(1, s, 0)

        def end(self):
            for way in (0, 1):
                for part in (0, 1):
                    self.wait(way, 3, part)
            return (
                self.pair(z, 2)
                + self.recv[0][3].astype(F32)
                + self.recv[1][3].astype(F32)
            )

    sum_r = Scatter(0, part_r, sib_r, precv_r, mrecv_r)
    sum_s = Scatter(1, part_s, sib_s, precv_s, mrecv_s)

    def scaled(w, bit, scale):
        code = lax.shift_right_arithmetic(lax.shift_left(w, I32(28 - bit)), I32(28))
        return (code.astype(F32) * scale).astype(BF16)

    def digits(words, scale_of, store):
        w = words.astype(I32) ^ 0x88888
        for k in range(5):
            store(k, scaled(w, 4 * k, scale_of(k)))

    def unpack_routed(b):
        local_gu[b].wait()

        def one(i, _):
            inner = i * 16
            for m in (0, 1):

                def scale_of(k):
                    return gu_scales[5 * b + k, pl.ds(m, 1), :]

                def store(k, value):
                    rows = pl.ds(al((5 * b + k) * 128 + inner, 16), 16)
                    weights[rows, m * HID : (m + 1) * HID] = value

                digits(rgu[m, pl.ds(al(128 * b + inner, 16), 16), :], scale_of, store)
            return 0

        lax.fori_loop(0, 8, one, 0)

    def routed_blocks(blocks):
        def one(j, _):
            rows = pl.ds(al(BLK * pick(j, blocks), 16), BLK)
            acc_r[...] += jnp.dot(
                xs_t[rows, :].T, weights[rows, :], preferred_element_type=F32
            )
            return 0

        lax.fori_loop(0, len(blocks), one, 0)

    def shared_shards(shards_in, place):
        def one(j, _):
            ee = pick(j, shards_in)
            first_row = BLK * (place + j)

            def strip(i, _):
                s = 5 * ee + i
                b = s // 8
                inner = lax.rem(s, 8) * 16
                at = first_row + i * 16
                for k in range(5):
                    xperm[pl.ds(al(k * 80 + at, 16), 16), :] = tk_t[
                        pl.ds(al((5 * b + k) * 128 + inner, 16), 16), :
                    ]
                words = pl.ds(al(s * 16, 16), 16)
                w0 = packed[0, words, :]
                w1 = packed[1, words, :]
                for k in range(5):
                    rows = pl.ds(al(k * 80 + at, 16), 16)
                    gate_scale = sgu_scales[5 * b + k, pl.ds(0, 1), :]
                    up_scale = sgu_scales[5 * b + k, pl.ds(1, 1), :]
                    wshard[rows, 0:HID] = scaled(w0, 4 * k, gate_scale)
                    wshard[rows, HID : 2 * HID] = (
                        scaled(w0, 20 + 4 * k, up_scale)
                        if k < 3
                        else scaled(w1, 4 * (k - 3), up_scale)
                    )
                return 0

            lax.fori_loop(0, 5, strip, 0)
            return 0

        lax.fori_loop(0, len(shards_in), one, 0)

    def shared_dot(count):
        rows = pl.ds(0, BLK * count)
        acc_s[...] += jnp.dot(xperm[rows, :].T, wshard[rows, :], preferred_element_type=F32)

    def activate(acc, target):
        g = acc[:, 0:HID]
        h = g / (1.0 + jnp.exp(-g)) * acc[:, HID : 2 * HID]
        target[...] = h.astype(BF16)

    def unpack_down(words, rows_of_scales, target):
        def strip(q, _):
            at = pl.ds(al(q * 16, 16), 16)

            def store(k, value):
                target[pl.ds(al(k * 128 + q * 16, 16), 16), :] = value

            digits(words(at), rows_of_scales, store)
            return 0

        lax.fori_loop(0, 8, strip, 0)

    def routed_chunks(chunks):
        def one(j, _):
            cols = pl.ds(al(HID * pick(j, chunks), 128), HID)
            unpack_down(lambda at: rdn[at, cols], lambda k: dn_scales[k, :, cols], wchunk)
            y = jnp.dot(hid_r[...], wchunk[...], preferred_element_type=F32)
            part_r[cols, :] = y.astype(BF16).T
            return 0

        lax.fori_loop(0, len(chunks), one, 0)

    def shared_chunks(chunks):
        def one(j, _):
            cols = pl.ds(al(HID * pick(j, chunks), 128), HID)
            at = al(128 * pick(j, chunks), 128)
            for r in range(16):
                for c in range(5):
                    turn_in[pl.ds(8 * (5 * r + c), 8), :] = packed[
                        1, pl.ds(al(at + 8 * r, 8), 8), pl.ds(128 * c, 128)
                    ]
            turned[...] = turn_in[...].T

            def strip(q, _):
                w = turned[pl.ds(al(q * 16, 16), 16), :]
                for k in range(5):
                    value = scaled(w, 8 + 4 * k, sdn_scales[pl.ds(k, 1), cols])
                    wchunk[pl.ds(al(k * 128 + q * 16, 16), 16), :] = value
                return 0

            lax.fori_loop(0, 8, strip, 0)
            y = jnp.dot(hid_s[...], wchunk[...], preferred_element_type=F32)
            part_s[cols, :] = y.astype(BF16).T
            return 0

        lax.fori_loop(0, len(chunks), one, 0)

    local_tok.wait()
    local_ids.wait()
    expert_row = ids[...]
    onehot = (lax.broadcasted_iota(I32, (16, TOK), 0) == expert_row).astype(F32)
    upto = (
        lax.broadcasted_iota(I32, (TOK, TOK), 0) <= lax.broadcasted_iota(I32, (TOK, TOK), 1)
    ).astype(BF16)
    counted = jnp.dot(onehot.astype(BF16), upto, preferred_element_type=F32)
    rank = jnp.sum(counted * onehot, axis=0, keepdims=True) - 1.0
    slot = expert_row.astype(F32) * 16.0 + rank
    chosen = lax.broadcasted_iota(I32, (SLOTS, TOK), 0).astype(F32) == slot
    select[...] = chosen.astype(F32).astype(BF16)
    disp[...] = lax.dot_general(
        select[...], tk_t[own_rows, :], (((1,), (1,)), ((), ())), preferred_element_type=F32
    ).astype(BF16)
    local_sgu.wait()
    local_sdn.wait()
    local_gs.wait()
    pack_own()

    def a2a(src, dst, k):
        def one(i, _):
            to = lax.rem(exp + i, 16)
            copy(
                src.at[pl.ds(al(16 * to, 16), 16), :],
                dst.at[pl.ds(al(16 * exp, 16), 16), :],
                asend.at[k],
                arecv.at[k],
                {"expert": to},
            ).start()
            return 0

        lax.fori_loop(1, 16, one, 0)
        mine = pl.ds(al(16 * exp, 16), 16)
        dst[mine, :] = src[mine, :]

    def a2a_wait(dst, k):
        ref = dst.at[pl.ds(0, 240), :]
        copy(ref, ref, asend.at[k], arecv.at[k], {"seq": other}).wait_recv()

    def a2a_end(src, k):
        ref = src.at[pl.ds(0, 240), :]
        copy(ref, ref, asend.at[k], arecv.at[k], {"seq": other}).wait_send()

    acc_r[...] = jnp.zeros(acc_r.shape, F32)
    acc_s[...] = jnp.zeros(acc_s.shape, F32)
    unpack_routed(0)
    unpack_routed(1)
    pl.semaphore_wait(barrier, 18)

    first = BLK * lax.rem(z + 4, NZ) // HID

    def chunks_for(offsets, chunks, total):
        qs = [lax.rem(first + q, 5) for q in offsets]
        chunks([5 * other + q for q in qs])
        for q in qs:
            cp = total.sibling_copy(HID * q, HID, q)
            cp.start()
            sent.append(cp)
        chunks([5 * core + q for q in qs])

    def chunks_wait(offsets, total):
        for q in offsets:
            at = lax.rem(first + q, 5)
            total.sibling_wait(HID * at, HID, at)

    def hidden_pair(c, r):
        if c is other:
            slots.sibling_wait(r)
            slots.sibling_wait(-r)
        routed_blocks([block_of(c, r), block_of(c, -r)])

    a2a(disp, disp_in, 0)
    toks.start_whole()
    low.r0()
    high.r0()
    unpack_routed(2)
    unpack_routed(3)
    unpack_routed(4)
    toks.step_whole(1)
    unpack_routed(5)
    unpack_routed(6)
    a2a_wait(disp_in, 0)
    xs_t[own_rows, :] = disp_in[...].T
    slots.start(True)
    unpack_routed(7)
    toks.step_whole(2)
    unpack_routed(8)
    slots.start(False)
    unpack_routed(9)
    local_ss.wait()
    local_sds.wait()
    toks.step_whole(3)
    low.r1()
    high.r1()
    slots.step(1, True)
    slots.sibling_wait(0)
    routed_blocks([block_of(core, 0), block_of(other, 0)])
    toks.step_whole(4)
    slots.step(1, False)
    hidden_pair(core, 1)
    for dz in (0, 1, -1, 2, -2, 3, -3, 4):
        toks.sibling_wait(dz)
    shared_shards(low.arrived(0), 0)
    slots.step(2, True)
    hidden_pair(other, 1)
    shared_shards(low.arrived(1)[0:1], 1)
    slots.step(2, False)
    hidden_pair(core, 2)
    shared_shards(low.arrived(1)[1:3], 2)
    slots.step(3, True)
    hidden_pair(other, 2)
    shared_shards(low.arrived(1)[3:4], 4)
    slots.step(3, False)
    hidden_pair(core, 3)
    low.r2()
    high.r2()
    slots.step(4, True)
    hidden_pair(other, 3)
    slots.sibling_wait(4)
    routed_blocks([block_of(core, 4), block_of(other, 4)])
    activate(acc_r, hid_r)
    local_ds.wait()
    local_dn.wait()
    chunks_for((0, 1), routed_chunks, sum_r)
    chunks_wait((0, 1), sum_r)
    sum_r.long_step(0)
    chunks_for((4, 2), routed_chunks, sum_r)
    chunks_wait((4, 2), sum_r)
    sum_r.short_step(1)
    sum_r.long_step(1)
    low.r3()
    high.r3()
    shared_dot(5)
    chunks_for((3,), routed_chunks, sum_r)
    low.r4()
    high.r4()
    chunks_wait((3,), sum_r)
    shared_shards(low.arrived(2)[0:1], 0)
    sum_r.short_step(2)
    shared_shards(low.arrived(2)[1:3], 1)
    sum_r.long_step(2)
    shared_shards(low.arrived(2)[3:6], 3)
    sum_r.short_step(3)
    shared_dot(6)
    sum_r.long_step(3)
    shared_shards(low.arrived(3), 0)
    shared_shards(low.arrived(4), 4)
    shared_dot(5)
    activate(acc_s, hid_s)
    chunks_for((0, 1), shared_chunks, sum_s)
    chunks_wait((0, 1), sum_s)
    sum_s.long_step(0)
    back[...] = sum_r.end().astype(BF16).T
    a2a(back, back_in, 1)
    chunks_for((4, 2), shared_chunks, sum_s)
    chunks_wait((4, 2), sum_s)
    sum_s.short_step(1)
    sum_s.long_step(1)
    chunks_for((3,), shared_chunks, sum_s)
    chunks_wait((3,), sum_s)
    sum_s.short_step(2)
    sum_s.long_step(2)
    drain(60)
    sum_s.short_step(3)
    sum_s.long_step(3)
    drain(12)
    a2a_end(disp, 0)
    a2a_end(back, 1)
    a2a_wait(back_in, 1)
    local_gate.wait()
    routed = lax.dot_general(
        back_in[...], select[...], (((0,), (0,)), ((), ())), preferred_element_type=F32
    )
    out[...] = (sum_s.end() + gate_w[...] * routed).astype(BF16)

    drain(0)


def shards(
    tokens,
    expert_ids,
    gate_weights,
    gate_up_codes,
    gate_up_scales,
    down_codes,
    down_scales,
    shared_gate_up_codes,
    shared_gate_up_scales,
    shared_down_codes,
    shared_down_scales,
):
    hbm = pl.BlockSpec(memory_space=pl.ANY)
    V = pltpu.VMEM
    S = pltpu.SemaphoreType.DMA
    return pl.pallas_call(
        kernel,
        out_shape=jax.ShapeDtypeStruct((BLK, TOK), BF16),
        in_specs=[hbm] * 11,
        out_specs=pl.BlockSpec(memory_space=pltpu.VMEM),
        scratch_shapes=[
            V((1, TOK), I32),
            V((1, TOK), F32),
            V((50, 2, HID), F32),
            V((5, 1, D), F32),
            V((50, 2, HID), F32),
            V((5, D), F32),
            V((2, 1280, HID), F32),
            V((128, D), F32),
            V((2, 80, HID), F32),
            V((BLK, 128), F32),
            V((2, 1280, HID), I32),
            V((HID, 128), I32),
            V((D, 2 * HID), BF16),
            V((6 * BLK, 2 * HID), BF16),
            V((HID, HID), BF16),
            V((128, HID), I32),
            V((D, SLOTS), BF16),
            V((D, TOK), BF16),
            V((6 * BLK, TOK), BF16),
            V((SLOTS, 2 * HID), F32),
            V((TOK, 2 * HID), F32),
            V((SLOTS, HID), BF16),
            V((TOK, HID), BF16),
            V((D, SLOTS), BF16),
            V((D, TOK), BF16),
            V((3200, SLOTS), BF16),
            V((3200, TOK), BF16),
            V((4, BLK, SLOTS), BF16),
            V((4, BLK, SLOTS), BF16),
            V((4, BLK, TOK), BF16),
            V((4, BLK, TOK), BF16),
            V((SLOTS, TOK), BF16),
            V((SLOTS, BLK), BF16),
            V((SLOTS, BLK), BF16),
            V((SLOTS, BLK), BF16),
            V((SLOTS, BLK), BF16),
            S((40,)),
            S((40,)),
            S((64,)),
            S((64,)),
            S((2,)),
            S((2,)),
            S((48,)),
            S((48,)),
            S((20,)),
        ],
        compiler_params=pltpu.CompilerParams(
            collective_id=0, has_side_effects=True, vmem_limit_bytes=64 * 1024 * 1024 - 65536
        ),
    )(
        tokens.T,
        expert_ids.reshape(1, TOK),
        gate_weights.reshape(1, TOK),
        gate_up_codes[0],
        jnp.transpose(gate_up_scales[0], (1, 0, 2)),
        down_codes[0],
        jnp.transpose(down_scales, (1, 0, 2)),
        shared_gate_up_codes,
        jnp.transpose(shared_gate_up_scales, (1, 0, 2)),
        shared_down_codes.T,
        shared_down_scales,
    ).T


def solution(mesh):
    placed = (
        P("expert", ("seq", "tensor")),
        P("expert"),
        P("expert"),
        P("expert", None, None, ("seq", "tensor")),
        P("expert", None, None, ("seq", "tensor")),
        P("expert", ("seq", "tensor"), None),
        P("expert", ("seq", "tensor"), None),
        P(None, "expert", ("seq", "tensor")),
        P(None, None, ("seq", "tensor")),
        P(("seq", "tensor"), "expert"),
        P(("seq", "tensor"), None),
    )
    return jax.shard_map(
        shards,
        mesh=mesh,
        in_specs=placed,
        out_specs=P("expert", ("seq", "tensor")),
        check_vma=False,
    )
```

```python
import jax
import jax.numpy as jnp
from jax import lax
from jax.experimental import pallas as pl
from jax.experimental.pallas import tpu as pltpu
from jax.sharding import PartitionSpec as P

MESH = pl.DeviceIdType.MESH
F32 = jnp.float32
BF16 = jnp.bfloat16
I32 = jnp.int32

D = 6400
HID = 640
SLOTS = 256
TOK = 128
BLK = 400
PARTS = ((0, 208), (208, 192), (0, 400))
NZ = 8


def al(value, multiple):
    return pl.multiple_of(value, multiple)


def pick(j, values):
    chosen = values[0]
    for k in range(1, len(values)):
        chosen = lax.select(j == k, values[k], chosen)
    return chosen


def kernel(
    tokens,
    ids_in,
    gate_in,
    gu_codes,
    gu_scales_in,
    dn_codes,
    dn_scales_in,
    sgu_codes,
    sgu_scales_in,
    sdn_codes,
    sdn_scales_in,
    out,
    ids,
    gate_w,
    gu_scales,
    dn_scales,
    sgu_scales,
    sdn_scales,
    rgu,
    rdn,
    own_gu,
    own_dn,
    packed,
    turn_in,
    weights,
    wshard,
    wchunk,
    turned,
    xs_t,
    tk_t,
    xperm,
    acc_r,
    acc_s,
    hid_r,
    hid_s,
    part_r,
    part_s,
    sib_r,
    sib_s,
    precv_r,
    mrecv_r,
    precv_s,
    mrecv_s,
    select,
    disp,
    disp_in,
    back,
    back_in,
    wsend,
    wrecv,
    zsend,
    zrecv,
    asend,
    arecv,
    rsend,
    rrecv,
    lsem,
):
    core = lax.axis_index("seq")
    exp = lax.axis_index("expert")
    z = lax.axis_index("tensor")
    ex = exp // 4
    ey = lax.rem(exp, 4)
    other = 1 - core
    zplus = lax.rem(z + 1, NZ)
    zminus = lax.rem(z + NZ - 1, NZ)

    barrier = pltpu.get_barrier_semaphore()

    def greet(k, _):
        pl.semaphore_signal(
            barrier, inc=1, device_id={"expert": lax.rem(exp + k, 16)}, device_id_type=MESH
        )
        return 0

    pl.semaphore_signal(barrier, inc=1, device_id={"seq": other}, device_id_type=MESH)
    pl.semaphore_signal(barrier, inc=1, device_id={"tensor": zplus}, device_id_type=MESH)
    pl.semaphore_signal(barrier, inc=1, device_id={"tensor": zminus}, device_id_type=MESH)
    lax.fori_loop(1, 16, greet, 0)

    def load(src, dst, k):
        cp = pltpu.make_async_copy(src, dst, lsem.at[k])
        cp.start()
        return cp

    own_rows = pl.ds(al(3200 * core + BLK * z, 16), BLK)
    local_tok = load(tokens, tk_t.at[own_rows, :], 0)
    local_ids = load(ids_in, ids, 1)
    local_gate = load(gate_in, gate_w, 2)
    local_sgu = load(sgu_codes, own_gu, 3)
    local_sdn = load(sdn_codes, own_dn, 4)
    local_gs = load(gu_scales_in, gu_scales, 5)
    local_gu = []
    for b in range(10):
        rows = pl.ds(128 * b, 128)
        local_gu.append(load(gu_codes.at[:, rows, :], rgu.at[:, rows, :], 10 + b))
    local_dn = load(dn_codes, rdn, 6)
    local_ds = load(dn_scales_in, dn_scales, 7)
    local_ss = load(sgu_scales_in, sgu_scales, 8)
    local_sds = load(sdn_scales_in, sdn_scales, 9)

    sent = []

    def copy(src, dst, ssem, rsem, device):
        return pltpu.make_async_remote_copy(
            src_ref=src,
            dst_ref=dst,
            send_sem=ssem,
            recv_sem=rsem,
            device_id=device,
            device_id_type=MESH,
        )

    def push(src, dst, ssem, rsem, device):
        cp = copy(src, dst, ssem, rsem, device)
        cp.start()
        sent.append(cp)

    def drain(keep):
        while len(sent) > keep:
            sent.pop(0).wait_send()

    def pack_own():
        for r in range(10):
            for c in range(5):
                rows, cols = pl.ds(8 * r, 8), pl.ds(128 * c, 128)
                g = own_gu[0, rows, cols].astype(I32)
                u = own_gu[1, rows, cols].astype(I32)
                d = own_dn[pl.ds(8 * (5 * r + c), 8), :].astype(I32)
                low = (g | lax.shift_left(u, I32(20))) ^ I32(-0x77777778)
                high = (lax.shift_right_logical(u, I32(12)) | lax.shift_left(d, I32(8))) ^ I32(0x08888888)
                at = pl.ds(al(80 * exp + 8 * r, 8), 8)
                packed[0, at, cols] = low
                packed[1, at, cols] = high

    def region(piece, ee, half):
        off, size = ((0, 80), (0, 40), (40, 40))[half]
        return packed.at[piece, pl.ds(al(80 * ee + off, 8), size), :]

    class Piece:
        def __init__(self, piece):
            self.piece = piece
            self.by_x = piece % 2 == 0
            self.a = ex if self.by_x else ey
            self.b = ey if self.by_x else ex

        def block(self, da, db):
            a = lax.rem(self.a + da + 4, 4)
            b = lax.rem(self.b + db + 4, 4)
            return a * 4 + b if self.by_x else b * 4 + a

        def send(self, sem, da, db, half, step_a, step_b):
            ref = region(self.piece, self.block(da, db), half)
            s = 20 * self.piece + sem
            push(ref, ref, wsend.at[s], wrecv.at[s], {"expert": self.block(step_a, step_b)})

        def wait(self, sem, da, db, half):
            ref = region(self.piece, self.block(da, db), half)
            s = 20 * self.piece + sem
            copy(ref, ref, wsend.at[s], wrecv.at[s], {"expert": self.block(1, 0)}).wait_recv()

        def stage2(self, q, da):
            self.send(4 + 4 * q, da, 0, 0, 0, 1)
            self.send(5 + 4 * q, da, 0, 0, 0, -1)

        def stage2_forward(self, q, da):
            self.wait(4 + 4 * q, da, -1, 0)
            self.send(6 + 4 * q, da, -1, 1, 0, 1)
            self.wait(5 + 4 * q, da, 1, 0)
            self.send(7 + 4 * q, da, 1, 2, 0, -1)

        def stage2_end(self, q, da):
            self.wait(6 + 4 * q, da, 2, 1)
            self.wait(7 + 4 * q, da, 2, 2)

        def r0(self):
            self.send(0, 0, 0, 0, 1, 0)
            self.send(1, 0, 0, 0, -1, 0)
            self.stage2(0, 0)

        def r1(self):
            self.wait(0, -1, 0, 0)
            self.send(2, -1, 0, 1, 1, 0)
            self.stage2(1, -1)
            self.wait(1, 1, 0, 0)
            self.send(3, 1, 0, 2, -1, 0)
            self.stage2(2, 1)
            self.stage2_forward(0, 0)

        def r2(self):
            self.wait(2, 2, 0, 1)
            self.wait(3, 2, 0, 2)
            self.stage2(3, 2)
            self.stage2_forward(1, -1)
            self.stage2_forward(2, 1)
            self.stage2_end(0, 0)

        def r3(self):
            self.stage2_forward(3, 2)
            self.stage2_end(1, -1)
            self.stage2_end(2, 1)

        def r4(self):
            self.stage2_end(3, 2)

        def arrived(self, r):
            places = (
                ((0, 0),),
                ((-1, 0), (1, 0), (0, -1), (0, 1)),
                ((2, 0), (0, 2), (-1, -1), (-1, 1), (1, -1), (1, 1)),
                ((2, -1), (2, 1), (-1, 2), (1, 2)),
                ((2, 2),),
            )[r]
            return [self.block(da, db) for da, db in places]

    low, high = Piece(0), Piece(1)

    def block_of(c, dz):
        return NZ * c + lax.rem(z + dz + NZ, NZ)

    class Gather:
        def __init__(self, ref, which):
            self.ref = ref
            self.base = 32 * which

        def rows(self, c, dz, part):
            off, size = PARTS[part]
            return self.ref.at[pl.ds(al(BLK * block_of(c, dz) + off, 16), size), :]

        def ring(self, up_way, r, part):
            ref = self.rows(core, -r if up_way else r, part)
            k = self.base + (0 if up_way else 8) + 2 * r + part % 2
            to = zplus if up_way else zminus
            push(ref, ref, zsend.at[k], zrecv.at[k], {"tensor": to})

        def sibling(self, dz):
            ref = self.rows(core, dz, 2)
            k = self.base + 16 + dz % NZ
            push(ref, ref, zsend.at[k], zrecv.at[k], {"seq": other})

        def ring_wait(self, up_way, r, part):
            ref = self.rows(core, -r if up_way else r, part)
            k = self.base + (0 if up_way else 8) + 2 * (r - 1) + part % 2
            copy(ref, ref, zsend.at[k], zrecv.at[k], {"tensor": zplus}).wait_recv()

        def sibling_wait(self, dz):
            ref = self.rows(other, dz, 2)
            k = self.base + 16 + dz % NZ
            copy(ref, ref, zsend.at[k], zrecv.at[k], {"seq": other}).wait_recv()

        def start(self, long_way):
            part = 0 if long_way else 1
            self.ring(True, 0, part)
            self.ring(False, 0, 1 - part)
            if long_way:
                self.sibling(0)

        def step(self, r, long_way):
            for up_way in (True, False):
                part = 0 if long_way == up_way else 1
                self.ring_wait(up_way, r, part)
                if r <= (3 if long_way else 2):
                    self.ring(up_way, r, part)
                if not long_way:
                    self.sibling(-r if up_way else r)
            if r == 4:
                self.sibling(4)

        def start_whole(self):
            self.ring(True, 0, 2)
            self.ring(False, 0, 2)
            self.sibling(0)

        def step_whole(self, r):
            self.ring_wait(True, r, 2)
            if r <= 3:
                self.ring(True, r, 2)
            self.sibling(-r)
            if r <= 3:
                self.ring_wait(False, r, 2)
                if r <= 2:
                    self.ring(False, r, 2)
                self.sibling(r)

    slots = Gather(xs_t, 0)
    toks = Gather(tk_t, 1)

    class Scatter:
        def __init__(self, which, part, sib, precv, mrecv):
            self.base = 24 * which
            self.part, self.sib = part, sib
            self.recv = (precv, mrecv)

        def sibling_copy(self, at, size, k):
            return copy(
                self.part.at[pl.ds(al(3200 * other + at, 16), size), :],
                self.sib.at[pl.ds(al(at, 16), size), :],
                rsend.at[self.base + k],
                rrecv.at[self.base + k],
                {"seq": other},
            )

        def sibling_wait(self, at, size, k):
            ref = self.sib.at[pl.ds(al(at, 16), size), :]
            k = self.base + k
            copy(ref, ref, rsend.at[k], rrecv.at[k], {"seq": other}).wait_recv()

        def pair(self, d, part):
            lo, size = PARTS[part]
            mine = self.part[pl.ds(al(BLK * (NZ * core + d) + lo, 16), size), :]
            theirs = self.sib[pl.ds(al(BLK * d + lo, 16), size), :]
            return mine.astype(F32) + theirs.astype(F32)

        def slot(self, way, s, part):
            lo, size = PARTS[part]
            return self.recv[way].at[s, pl.ds(lo, size), :]

        def wait(self, way, s, part):
            ref = self.slot(way, s, part)
            k = self.base + 8 + 8 * way + 2 * s + part
            copy(ref, ref, rsend.at[k], rrecv.at[k], {"tensor": zplus}).wait_recv()

        def message(self, way, s, part):
            lo, size = PARTS[part]
            d = lax.rem(z + (4 - s if way == 0 else s - 4) + NZ, NZ)
            value = self.pair(d, part)
            if s > (0 if way == part else 1):
                self.wait(way, s - 1, part)
                value = value + self.recv[way][s - 1, pl.ds(lo, size), :].astype(F32)
            rows = pl.ds(al(BLK * (NZ * core + d) + lo, 16), size)
            self.part[rows, :] = value.astype(BF16)
            k = self.base + 8 + 8 * way + 2 * s + part
            push(
                self.part.at[rows, :],
                self.slot(way, s, part),
                rsend.at[k],
                rrecv.at[k],
                {"tensor": zplus if way == 0 else zminus},
            )

        def long_step(self, s):
            self.message(0, s, 0)
            self.message(1, s, 1)

        def short_step(self, s):
            self.message(0, s, 1)
            self.message(1, s, 0)

        def end(self):
            for way in (0, 1):
                for part in (0, 1):
                    self.wait(way, 3, part)
            return (
                self.pair(z, 2)
                + self.recv[0][3].astype(F32)
                + self.recv[1][3].astype(F32)
            )

    sum_r = Scatter(0, part_r, sib_r, precv_r, mrecv_r)
    sum_s = Scatter(1, part_s, sib_s, precv_s, mrecv_s)

    def scaled(w, bit, scale):
        code = lax.shift_right_arithmetic(lax.shift_left(w, I32(28 - bit)), I32(28))
        return (code.astype(F32) * scale).astype(BF16)

    def digits(words, scale_of, store):
        w = words.astype(I32) ^ 0x88888
        for k in range(5):
            store(k, scaled(w, 4 * k, scale_of(k)))

    def unpack_routed(b):
        local_gu[b].wait()

        def one(i, _):
            inner = i * 16
            for m in (0, 1):

                def scale_of(k):
                    return gu_scales[5 * b + k, pl.ds(m, 1), :]

                def store(k, value):
                    rows = pl.ds(al((5 * b + k) * 128 + inner, 16), 16)
                    weights[rows, m * HID : (m + 1) * HID] = value

                digits(rgu[m, pl.ds(al(128 * b + inner, 16), 16), :], scale_of, store)
            return 0

        lax.fori_loop(0, 8, one, 0)

    def routed_blocks(blocks):
        def one(j, _):
            rows = pl.ds(al(BLK * pick(j, blocks), 16), BLK)
            acc_r[...] += jnp.dot(
                xs_t[rows, :].T, weights[rows, :], preferred_element_type=F32
            )
            return 0

        lax.fori_loop(0, len(blocks), one, 0)

    def shared_shards(shards_in, place):
        def one(j, _):
            ee = pick(j, shards_in)
            first_row = BLK * (place + j)

            def strip(i, _):
                s = 5 * ee + i
                b = s // 8
                inner = lax.rem(s, 8) * 16
                at = first_row + i * 16
                for k in range(5):
                    xperm[pl.ds(al(k * 80 + at, 16), 16), :] = tk_t[
                        pl.ds(al((5 * b + k) * 128 + inner, 16), 16), :
                    ]
                words = pl.ds(al(s * 16, 16), 16)
                w0 = packed[0, words, :]
                w1 = packed[1, words, :]
                for k in range(5):
                    rows = pl.ds(al(k * 80 + at, 16), 16)
                    gate_scale = sgu_scales[5 * b + k, pl.ds(0, 1), :]
                    up_scale = sgu_scales[5 * b + k, pl.ds(1, 1), :]
                    wshard[rows, 0:HID] = scaled(w0, 4 * k, gate_scale)
                    wshard[rows, HID : 2 * HID] = (
                        scaled(w0, 20 + 4 * k, up_scale)
                        if k < 3
                        else scaled(w1, 4 * (k - 3), up_scale)
                    )
                return 0

            lax.fori_loop(0, 5, strip, 0)
            return 0

        lax.fori_loop(0, len(shards_in), one, 0)

    def shared_dot(count):
        rows = pl.ds(0, BLK * count)
        acc_s[...] += jnp.dot(xperm[rows, :].T, wshard[rows, :], preferred_element_type=F32)

    def activate(acc, target):
        g = acc[:, 0:HID]
        h = g / (1.0 + jnp.exp(-g)) * acc[:, HID : 2 * HID]
        target[...] = h.astype(BF16)

    def unpack_down(words, rows_of_scales, target):
        def strip(q, _):
            at = pl.ds(al(q * 16, 16), 16)

            def store(k, value):
                target[pl.ds(al(k * 128 + q * 16, 16), 16), :] = value

            digits(words(at), rows_of_scales, store)
            return 0

        lax.fori_loop(0, 8, strip, 0)

    def routed_chunks(chunks):
        def one(j, _):
            cols = pl.ds(al(HID * pick(j, chunks), 128), HID)
            unpack_down(lambda at: rdn[at, cols], lambda k: dn_scales[k, :, cols], wchunk)
            y = jnp.dot(hid_r[...], wchunk[...], preferred_element_type=F32)
            part_r[cols, :] = y.astype(BF16).T
            return 0

        lax.fori_loop(0, len(chunks), one, 0)

    def shared_chunks(chunks):
        def one(j, _):
            cols = pl.ds(al(HID * pick(j, chunks), 128), HID)
            at = al(128 * pick(j, chunks), 128)
            for r in range(16):
                for c in range(5):
                    turn_in[pl.ds(8 * (5 * r + c), 8), :] = packed[
                        1, pl.ds(al(at + 8 * r, 8), 8), pl.ds(128 * c, 128)
                    ]
            turned[...] = turn_in[...].T

            def strip(q, _):
                w = turned[pl.ds(al(q * 16, 16), 16), :]
                for k in range(5):
                    value = scaled(w, 8 + 4 * k, sdn_scales[pl.ds(k, 1), cols])
                    wchunk[pl.ds(al(k * 128 + q * 16, 16), 16), :] = value
                return 0

            lax.fori_loop(0, 8, strip, 0)
            y = jnp.dot(hid_s[...], wchunk[...], preferred_element_type=F32)
            part_s[cols, :] = y.astype(BF16).T
            return 0

        lax.fori_loop(0, len(chunks), one, 0)

    local_tok.wait()
    local_ids.wait()
    expert_row = ids[...]
    onehot = (lax.broadcasted_iota(I32, (16, TOK), 0) == expert_row).astype(F32)
    upto = (
        lax.broadcasted_iota(I32, (TOK, TOK), 0) <= lax.broadcasted_iota(I32, (TOK, TOK), 1)
    ).astype(BF16)
    counted = jnp.dot(onehot.astype(BF16), upto, preferred_element_type=F32)
    rank = jnp.sum(counted * onehot, axis=0, keepdims=True) - 1.0
    slot = expert_row.astype(F32) * 16.0 + rank
    chosen = lax.broadcasted_iota(I32, (SLOTS, TOK), 0).astype(F32) == slot
    select[...] = chosen.astype(F32).astype(BF16)
    disp[...] = lax.dot_general(
        select[...], tk_t[own_rows, :], (((1,), (1,)), ((), ())), preferred_element_type=F32
    ).astype(BF16)
    local_sgu.wait()
    local_sdn.wait()
    local_gs.wait()
    pack_own()

    def a2a(src, dst, k):
        def one(i, _):
            to = lax.rem(exp + i, 16)
            copy(
                src.at[pl.ds(al(16 * to, 16), 16), :],
                dst.at[pl.ds(al(16 * exp, 16), 16), :],
                asend.at[k],
                arecv.at[k],
                {"expert": to},
            ).start()
            return 0

        lax.fori_loop(1, 16, one, 0)
        mine = pl.ds(al(16 * exp, 16), 16)
        dst[mine, :] = src[mine, :]

    def a2a_wait(dst, k):
        ref = dst.at[pl.ds(0, 240), :]
        copy(ref, ref, asend.at[k], arecv.at[k], {"seq": other}).wait_recv()

    def a2a_end(src, k):
        ref = src.at[pl.ds(0, 240), :]
        copy(ref, ref, asend.at[k], arecv.at[k], {"seq": other}).wait_send()

    acc_r[...] = jnp.zeros(acc_r.shape, F32)
    acc_s[...] = jnp.zeros(acc_s.shape, F32)
    unpack_routed(0)
    unpack_routed(1)
    pl.semaphore_wait(barrier, 18)

    first = BLK * lax.rem(z + 4, NZ) // HID

    def chunks_for(offsets, chunks, total):
        qs = [lax.rem(first + q, 5) for q in offsets]
        chunks([5 * other + q for q in qs])
        for q in qs:
            cp = total.sibling_copy(HID * q, HID, q)
            cp.start()
            sent.append(cp)
        chunks([5 * core + q for q in qs])

    def chunks_wait(offsets, total):
        for q in offsets:
            at = lax.rem(first + q, 5)
            total.sibling_wait(HID * at, HID, at)

    def hidden_pair(c, r):
        if c is other:
            slots.sibling_wait(r)
            slots.sibling_wait(-r)
        routed_blocks([block_of(c, r), block_of(c, -r)])

    a2a(disp, disp_in, 0)
    toks.start_whole()
    low.r0()
    high.r0()
    unpack_routed(2)
    unpack_routed(3)
    unpack_routed(4)
    toks.step_whole(1)
    unpack_routed(5)
    unpack_routed(6)
    a2a_wait(disp_in, 0)
    xs_t[own_rows, :] = disp_in[...].T
    slots.start(True)
    unpack_routed(7)
    toks.step_whole(2)
    unpack_routed(8)
    slots.start(False)
    unpack_routed(9)
    local_ss.wait()
    local_sds.wait()
    toks.step_whole(3)
    low.r1()
    high.r1()
    slots.step(1, True)
    slots.sibling_wait(0)
    routed_blocks([block_of(core, 0), block_of(other, 0)])
    toks.step_whole(4)
    slots.step(1, False)
    hidden_pair(core, 1)
    for dz in (0, 1, -1, 2, -2, 3, -3, 4):
        toks.sibling_wait(dz)
    shared_shards(low.arrived(0), 0)
    slots.step(2, True)
    hidden_pair(other, 1)
    shared_shards(low.arrived(1)[0:1], 1)
    slots.step(2, False)
    hidden_pair(core, 2)
    shared_shards(low.arrived(1)[1:3], 2)
    slots.step(3, True)
    hidden_pair(other, 2)
    shared_shards(low.arrived(1)[3:4], 4)
    slots.step(3, False)
    hidden_pair(core, 3)
    low.r2()
    high.r2()
    slots.step(4, True)
    hidden_pair(other, 3)
    slots.sibling_wait(4)
    routed_blocks([block_of(core, 4), block_of(other, 4)])
    activate(acc_r, hid_r)
    local_ds.wait()
    local_dn.wait()
    chunks_for((0, 1), routed_chunks, sum_r)
    chunks_wait((0, 1), sum_r)
    sum_r.long_step(0)
    shared_dot(5)
    chunks_for((4, 2), routed_chunks, sum_r)
    chunks_wait((4, 2), sum_r)
    sum_r.short_step(1)
    sum_r.long_step(1)
    low.r3()
    high.r3()
    chunks_for((3,), routed_chunks, sum_r)
    chunks_wait((3,), sum_r)
    shared_shards(low.arrived(2), 0)
    sum_r.short_step(2)
    low.r4()
    high.r4()
    sum_r.long_step(2)
    shared_dot(6)
    shared_shards(low.arrived(3) + low.arrived(4), 0)
    shared_dot(5)
    activate(acc_s, hid_s)
    sum_r.short_step(3)
    sum_r.long_step(3)
    chunks_for((0, 1), shared_chunks, sum_s)
    chunks_wait((0, 1), sum_s)
    sum_s.long_step(0)
    chunks_for((4, 2), shared_chunks, sum_s)
    chunks_wait((4, 2), sum_s)
    sum_s.short_step(1)
    sum_s.long_step(1)
    back[...] = sum_r.end().astype(BF16).T
    a2a(back, back_in, 1)
    chunks_for((3,), shared_chunks, sum_s)
    chunks_wait((3,), sum_s)
    sum_s.short_step(2)
    sum_s.long_step(2)
    drain(60)
    sum_s.short_step(3)
    sum_s.long_step(3)
    drain(12)
    a2a_end(disp, 0)
    a2a_end(back, 1)
    a2a_wait(back_in, 1)
    local_gate.wait()
    routed = lax.dot_general(
        back_in[...], select[...], (((0,), (0,)), ((), ())), preferred_element_type=F32
    )
    out[...] = (sum_s.end() + gate_w[...] * routed).astype(BF16)

    drain(0)


def shards(
    tokens,
    expert_ids,
    gate_weights,
    gate_up_codes,
    gate_up_scales,
    down_codes,
    down_scales,
    shared_gate_up_codes,
    shared_gate_up_scales,
    shared_down_codes,
    shared_down_scales,
):
    hbm = pl.BlockSpec(memory_space=pl.ANY)
    V = pltpu.VMEM
    S = pltpu.SemaphoreType.DMA
    return pl.pallas_call(
        kernel,
        out_shape=jax.ShapeDtypeStruct((BLK, TOK), BF16),
        in_specs=[hbm] * 11,
        out_specs=pl.BlockSpec(memory_space=pltpu.VMEM),
        scratch_shapes=[
            V((1, TOK), I32),
            V((1, TOK), F32),
            V((50, 2, HID), F32),
            V((5, 1, D), F32),
            V((50, 2, HID), F32),
            V((5, D), F32),
            V((2, 1280, HID), F32),
            V((128, D), F32),
            V((2, 80, HID), F32),
            V((BLK, 128), F32),
            V((2, 1280, HID), I32),
            V((HID, 128), I32),
            V((D, 2 * HID), BF16),
            V((6 * BLK, 2 * HID), BF16),
            V((HID, HID), BF16),
            V((128, HID), I32),
            V((D, SLOTS), BF16),
            V((D, TOK), BF16),
            V((6 * BLK, TOK), BF16),
            V((SLOTS, 2 * HID), F32),
            V((TOK, 2 * HID), F32),
            V((SLOTS, HID), BF16),
            V((TOK, HID), BF16),
            V((D, SLOTS), BF16),
            V((D, TOK), BF16),
            V((3200, SLOTS), BF16),
            V((3200, TOK), BF16),
            V((4, BLK, SLOTS), BF16),
            V((4, BLK, SLOTS), BF16),
            V((4, BLK, TOK), BF16),
            V((4, BLK, TOK), BF16),
            V((SLOTS, TOK), BF16),
            V((SLOTS, BLK), BF16),
            V((SLOTS, BLK), BF16),
            V((SLOTS, BLK), BF16),
            V((SLOTS, BLK), BF16),
            S((40,)),
            S((40,)),
            S((64,)),
            S((64,)),
            S((2,)),
            S((2,)),
            S((48,)),
            S((48,)),
            S((20,)),
        ],
        compiler_params=pltpu.CompilerParams(
            collective_id=0, has_side_effects=True, vmem_limit_bytes=64 * 1024 * 1024 - 65536
        ),
    )(
        tokens.T,
        expert_ids.reshape(1, TOK),
        gate_weights.reshape(1, TOK),
        gate_up_codes[0],
        jnp.transpose(gate_up_scales[0], (1, 0, 2)),
        down_codes[0],
        jnp.transpose(down_scales, (1, 0, 2)),
        shared_gate_up_codes,
        jnp.transpose(shared_gate_up_scales, (1, 0, 2)),
        shared_down_codes.T,
        shared_down_scales,
    ).T


def solution(mesh):
    placed = (
        P("expert", ("seq", "tensor")),
        P("expert"),
        P("expert"),
        P("expert", None, None, ("seq", "tensor")),
        P("expert", None, None, ("seq", "tensor")),
        P("expert", ("seq", "tensor"), None),
        P("expert", ("seq", "tensor"), None),
        P(None, "expert", ("seq", "tensor")),
        P(None, None, ("seq", "tensor")),
        P(("seq", "tensor"), "expert"),
        P(("seq", "tensor"), None),
    )
    return jax.shard_map(
        shards,
        mesh=mesh,
        in_specs=placed,
        out_specs=P("expert", ("seq", "tensor")),
        check_vma=False,
    )
```

```python
import jax
import jax.numpy as jnp
from jax import lax
from jax.experimental import pallas as pl
from jax.experimental.pallas import tpu as pltpu
from jax.sharding import PartitionSpec as P

MESH = pl.DeviceIdType.MESH
F32 = jnp.float32
BF16 = jnp.bfloat16
I32 = jnp.int32

D = 6400
HID = 640
SLOTS = 256
TOK = 128
BLK = 400
PARTS = ((0, 208), (208, 192), (0, 400))
NZ = 8


def al(value, multiple):
    return pl.multiple_of(value, multiple)


def pick(j, values):
    chosen = values[0]
    for k in range(1, len(values)):
        chosen = lax.select(j == k, values[k], chosen)
    return chosen


def kernel(
    tokens,
    ids_in,
    gate_in,
    gu_codes,
    gu_scales_in,
    dn_codes,
    dn_scales_in,
    sgu_codes,
    sgu_scales_in,
    sdn_codes,
    sdn_scales_in,
    out,
    ids,
    gate_w,
    gu_scales,
    dn_scales,
    sgu_scales,
    sdn_scales,
    rgu,
    rdn,
    own_gu,
    own_dn,
    packed,
    turn_in,
    weights,
    wshard,
    wchunk,
    turned,
    xs_t,
    tk_t,
    xperm,
    acc_r,
    acc_s,
    hid_r,
    hid_s,
    part_r,
    part_s,
    sib_r,
    sib_s,
    precv_r,
    mrecv_r,
    precv_s,
    mrecv_s,
    select,
    disp,
    disp_in,
    back,
    back_in,
    wsend,
    wrecv,
    zsend,
    zrecv,
    asend,
    arecv,
    rsend,
    rrecv,
    lsem,
):
    core = lax.axis_index("seq")
    exp = lax.axis_index("expert")
    z = lax.axis_index("tensor")
    ex = exp // 4
    ey = lax.rem(exp, 4)
    other = 1 - core
    zplus = lax.rem(z + 1, NZ)
    zminus = lax.rem(z + NZ - 1, NZ)

    barrier = pltpu.get_barrier_semaphore()

    def greet(k, _):
        pl.semaphore_signal(
            barrier, inc=1, device_id={"expert": lax.rem(exp + k, 16)}, device_id_type=MESH
        )
        return 0

    pl.semaphore_signal(barrier, inc=1, device_id={"seq": other}, device_id_type=MESH)
    pl.semaphore_signal(barrier, inc=1, device_id={"tensor": zplus}, device_id_type=MESH)
    pl.semaphore_signal(barrier, inc=1, device_id={"tensor": zminus}, device_id_type=MESH)
    lax.fori_loop(1, 16, greet, 0)

    def load(src, dst, k):
        cp = pltpu.make_async_copy(src, dst, lsem.at[k])
        cp.start()
        return cp

    own_rows = pl.ds(al(3200 * core + BLK * z, 16), BLK)
    local_tok = load(tokens, tk_t.at[own_rows, :], 0)
    local_ids = load(ids_in, ids, 1)
    local_gate = load(gate_in, gate_w, 2)
    local_sgu = load(sgu_codes, own_gu, 3)
    local_sdn = load(sdn_codes, own_dn, 4)
    local_gs = load(gu_scales_in, gu_scales, 5)
    local_gu = []
    for b in range(10):
        rows = pl.ds(128 * b, 128)
        local_gu.append(load(gu_codes.at[:, rows, :], rgu.at[:, rows, :], 10 + b))
    local_dn = load(dn_codes, rdn, 6)
    local_ds = load(dn_scales_in, dn_scales, 7)
    local_ss = load(sgu_scales_in, sgu_scales, 8)
    local_sds = load(sdn_scales_in, sdn_scales, 9)

    sent = []

    def copy(src, dst, ssem, rsem, device):
        return pltpu.make_async_remote_copy(
            src_ref=src,
            dst_ref=dst,
            send_sem=ssem,
            recv_sem=rsem,
            device_id=device,
            device_id_type=MESH,
        )

    def push(src, dst, ssem, rsem, device):
        cp = copy(src, dst, ssem, rsem, device)
        cp.start()
        sent.append(cp)

    def drain(keep):
        while len(sent) > keep:
            sent.pop(0).wait_send()

    def pack_own():
        for r in range(10):
            for c in range(5):
                rows, cols = pl.ds(8 * r, 8), pl.ds(128 * c, 128)
                g = own_gu[0, rows, cols].astype(I32)
                u = own_gu[1, rows, cols].astype(I32)
                d = own_dn[pl.ds(8 * (5 * r + c), 8), :].astype(I32)
                low = (g | lax.shift_left(u, I32(20))) ^ I32(-0x77777778)
                high = (lax.shift_right_logical(u, I32(12)) | lax.shift_left(d, I32(8))) ^ I32(0x08888888)
                at = pl.ds(al(80 * exp + 8 * r, 8), 8)
                packed[0, at, cols] = low
                packed[1, at, cols] = high

    def region(piece, ee, half):
        off, size = ((0, 80), (0, 40), (40, 40))[half]
        return packed.at[piece, pl.ds(al(80 * ee + off, 8), size), :]

    class Piece:
        def __init__(self, piece):
            self.piece = piece
            self.by_x = piece % 2 == 0
            self.a = ex if self.by_x else ey
            self.b = ey if self.by_x else ex

        def block(self, da, db):
            a = lax.rem(self.a + da + 4, 4)
            b = lax.rem(self.b + db + 4, 4)
            return a * 4 + b if self.by_x else b * 4 + a

        def send(self, sem, da, db, half, step_a, step_b):
            ref = region(self.piece, self.block(da, db), half)
            s = 20 * self.piece + sem
            push(ref, ref, wsend.at[s], wrecv.at[s], {"expert": self.block(step_a, step_b)})

        def wait(self, sem, da, db, half):
            ref = region(self.piece, self.block(da, db), half)
            s = 20 * self.piece + sem
            copy(ref, ref, wsend.at[s], wrecv.at[s], {"expert": self.block(1, 0)}).wait_recv()

        def stage2(self, q, da):
            self.send(4 + 4 * q, da, 0, 0, 0, 1)
            self.send(5 + 4 * q, da, 0, 0, 0, -1)

        def stage2_forward(self, q, da):
            self.wait(4 + 4 * q, da, -1, 0)
            self.send(6 + 4 * q, da, -1, 1, 0, 1)
            self.wait(5 + 4 * q, da, 1, 0)
            self.send(7 + 4 * q, da, 1, 2, 0, -1)

        def stage2_end(self, q, da):
            self.wait(6 + 4 * q, da, 2, 1)
            self.wait(7 + 4 * q, da, 2, 2)

        def r0(self):
            self.send(0, 0, 0, 0, 1, 0)
            self.send(1, 0, 0, 0, -1, 0)
            self.stage2(0, 0)

        def r1(self):
            self.wait(0, -1, 0, 0)
            self.send(2, -1, 0, 1, 1, 0)
            self.stage2(1, -1)
            self.wait(1, 1, 0, 0)
            self.send(3, 1, 0, 2, -1, 0)
            self.stage2(2, 1)
            self.stage2_forward(0, 0)

        def r2(self):
            self.wait(2, 2, 0, 1)
            self.wait(3, 2, 0, 2)
            self.stage2(3, 2)
            self.stage2_forward(1, -1)
            self.stage2_forward(2, 1)
            self.stage2_end(0, 0)

        def r3(self):
            self.stage2_forward(3, 2)
            self.stage2_end(1, -1)
            self.stage2_end(2, 1)

        def r4(self):
            self.stage2_end(3, 2)

        def arrived(self, r):
            places = (
                ((0, 0),),
                ((-1, 0), (1, 0), (0, -1), (0, 1)),
                ((2, 0), (0, 2), (-1, -1), (-1, 1), (1, -1), (1, 1)),
                ((2, -1), (2, 1), (-1, 2), (1, 2)),
                ((2, 2),),
            )[r]
            return [self.block(da, db) for da, db in places]

    low, high = Piece(0), Piece(1)

    def block_of(c, dz):
        return NZ * c + lax.rem(z + dz + NZ, NZ)

    class Gather:
        def __init__(self, ref, which):
            self.ref = ref
            self.base = 32 * which

        def rows(self, c, dz, part):
            off, size = PARTS[part]
            return self.ref.at[pl.ds(al(BLK * block_of(c, dz) + off, 16), size), :]

        def ring(self, up_way, r, part):
            ref = self.rows(core, -r if up_way else r, part)
            k = self.base + (0 if up_way else 8) + 2 * r + part % 2
            to = zplus if up_way else zminus
            push(ref, ref, zsend.at[k], zrecv.at[k], {"tensor": to})

        def sibling(self, dz):
            ref = self.rows(core, dz, 2)
            k = self.base + 16 + dz % NZ
            push(ref, ref, zsend.at[k], zrecv.at[k], {"seq": other})

        def ring_wait(self, up_way, r, part):
            ref = self.rows(core, -r if up_way else r, part)
            k = self.base + (0 if up_way else 8) + 2 * (r - 1) + part % 2
            copy(ref, ref, zsend.at[k], zrecv.at[k], {"tensor": zplus}).wait_recv()

        def sibling_wait(self, dz):
            ref = self.rows(other, dz, 2)
            k = self.base + 16 + dz % NZ
            copy(ref, ref, zsend.at[k], zrecv.at[k], {"seq": other}).wait_recv()

        def start(self, long_way):
            part = 0 if long_way else 1
            self.ring(True, 0, part)
            self.ring(False, 0, 1 - part)
            if long_way:
                self.sibling(0)

        def step(self, r, long_way):
            for up_way in (True, False):
                part = 0 if long_way == up_way else 1
                self.ring_wait(up_way, r, part)
                if r <= (3 if long_way else 2):
                    self.ring(up_way, r, part)
                if not long_way:
                    self.sibling(-r if up_way else r)
            if r == 4:
                self.sibling(4)

        def start_whole(self):
            self.ring(True, 0, 2)
            self.ring(False, 0, 2)
            self.sibling(0)

        def step_whole(self, r):
            self.ring_wait(True, r, 2)
            if r <= 3:
                self.ring(True, r, 2)
            self.sibling(-r)
            if r <= 3:
                self.ring_wait(False, r, 2)
                if r <= 2:
                    self.ring(False, r, 2)
                self.sibling(r)

    slots = Gather(xs_t, 0)
    toks = Gather(tk_t, 1)

    class Scatter:
        def __init__(self, which, part, sib, precv, mrecv):
            self.base = 24 * which
            self.part, self.sib = part, sib
            self.recv = (precv, mrecv)

        def sibling_copy(self, at, size, k):
            return copy(
                self.part.at[pl.ds(al(3200 * other + at, 16), size), :],
                self.sib.at[pl.ds(al(at, 16), size), :],
                rsend.at[self.base + k],
                rrecv.at[self.base + k],
                {"seq": other},
            )

        def sibling_wait(self, at, size, k):
            ref = self.sib.at[pl.ds(al(at, 16), size), :]
            k = self.base + k
            copy(ref, ref, rsend.at[k], rrecv.at[k], {"seq": other}).wait_recv()

        def pair(self, d, part):
            lo, size = PARTS[part]
            mine = self.part[pl.ds(al(BLK * (NZ * core + d) + lo, 16), size), :]
            theirs = self.sib[pl.ds(al(BLK * d + lo, 16), size), :]
            return mine.astype(F32) + theirs.astype(F32)

        def slot(self, way, s, part):
            lo, size = PARTS[part]
            return self.recv[way].at[s, pl.ds(lo, size), :]

        def wait(self, way, s, part):
            ref = self.slot(way, s, part)
            k = self.base + 8 + 8 * way + 2 * s + part
            copy(ref, ref, rsend.at[k], rrecv.at[k], {"tensor": zplus}).wait_recv()

        def message(self, way, s, part):
            lo, size = PARTS[part]
            d = lax.rem(z + (4 - s if way == 0 else s - 4) + NZ, NZ)
            value = self.pair(d, part)
            if s > (0 if way == part else 1):
                self.wait(way, s - 1, part)
                value = value + self.recv[way][s - 1, pl.ds(lo, size), :].astype(F32)
            rows = pl.ds(al(BLK * (NZ * core + d) + lo, 16), size)
            self.part[rows, :] = value.astype(BF16)
            k = self.base + 8 + 8 * way + 2 * s + part
            push(
                self.part.at[rows, :],
                self.slot(way, s, part),
                rsend.at[k],
                rrecv.at[k],
                {"tensor": zplus if way == 0 else zminus},
            )

        def long_step(self, s):
            self.message(0, s, 0)
            self.message(1, s, 1)

        def short_step(self, s):
            self.message(0, s, 1)
            self.message(1, s, 0)

        def end(self):
            for way in (0, 1):
                for part in (0, 1):
                    self.wait(way, 3, part)
            return (
                self.pair(z, 2)
                + self.recv[0][3].astype(F32)
                + self.recv[1][3].astype(F32)
            )

    sum_r = Scatter(0, part_r, sib_r, precv_r, mrecv_r)
    sum_s = Scatter(1, part_s, sib_s, precv_s, mrecv_s)

    def scaled(w, bit, scale):
        code = lax.shift_right_arithmetic(lax.shift_left(w, I32(28 - bit)), I32(28))
        return (code.astype(F32) * scale).astype(BF16)

    def digits(words, scale_of, store):
        w = words.astype(I32) ^ 0x88888
        for k in range(5):
            store(k, scaled(w, 4 * k, scale_of(k)))

    def unpack_routed(b):
        local_gu[b].wait()

        def one(i, _):
            inner = i * 16
            for m in (0, 1):

                def scale_of(k):
                    return gu_scales[5 * b + k, pl.ds(m, 1), :]

                def store(k, value):
                    rows = pl.ds(al((5 * b + k) * 128 + inner, 16), 16)
                    weights[rows, m * HID : (m + 1) * HID] = value

                digits(rgu[m, pl.ds(al(128 * b + inner, 16), 16), :], scale_of, store)
            return 0

        lax.fori_loop(0, 8, one, 0)

    def routed_blocks(blocks):
        def one(j, _):
            rows = pl.ds(al(BLK * pick(j, blocks), 16), BLK)
            acc_r[...] += jnp.dot(
                xs_t[rows, :].T, weights[rows, :], preferred_element_type=F32
            )
            return 0

        lax.fori_loop(0, len(blocks), one, 0, unroll=True)

    def shared_shards(shards_in, place):
        def one(j, _):
            ee = pick(j, shards_in)
            first_row = BLK * (place + j)

            def strip(i, _):
                s = 5 * ee + i
                b = s // 8
                inner = lax.rem(s, 8) * 16
                at = first_row + i * 16
                for k in range(5):
                    xperm[pl.ds(al(k * 80 + at, 16), 16), :] = tk_t[
                        pl.ds(al((5 * b + k) * 128 + inner, 16), 16), :
                    ]
                words = pl.ds(al(s * 16, 16), 16)
                w0 = packed[0, words, :]
                w1 = packed[1, words, :]
                for k in range(5):
                    rows = pl.ds(al(k * 80 + at, 16), 16)
                    gate_scale = sgu_scales[5 * b + k, pl.ds(0, 1), :]
                    up_scale = sgu_scales[5 * b + k, pl.ds(1, 1), :]
                    wshard[rows, 0:HID] = scaled(w0, 4 * k, gate_scale)
                    wshard[rows, HID : 2 * HID] = (
                        scaled(w0, 20 + 4 * k, up_scale)
                        if k < 3
                        else scaled(w1, 4 * (k - 3), up_scale)
                    )
                return 0

            lax.fori_loop(0, 5, strip, 0)
            return 0

        lax.fori_loop(0, len(shards_in), one, 0)

    def shared_dot(count):
        rows = pl.ds(0, BLK * count)
        acc_s[...] += jnp.dot(xperm[rows, :].T, wshard[rows, :], preferred_element_type=F32)

    def activate(acc, target):
        g = acc[:, 0:HID]
        h = g / (1.0 + jnp.exp(-g)) * acc[:, HID : 2 * HID]
        target[...] = h.astype(BF16)

    def unpack_down(words, rows_of_scales, target):
        def strip(q, _):
            at = pl.ds(al(q * 16, 16), 16)

            def store(k, value):
                target[pl.ds(al(k * 128 + q * 16, 16), 16), :] = value

            digits(words(at), rows_of_scales, store)
            return 0

        lax.fori_loop(0, 8, strip, 0, unroll=2)

    def routed_chunks(chunks):
        def one(j, _):
            cols = pl.ds(al(HID * pick(j, chunks), 128), HID)
            unpack_down(lambda at: rdn[at, cols], lambda k: dn_scales[k, :, cols], wchunk)
            y = jnp.dot(hid_r[...], wchunk[...], preferred_element_type=F32)
            part_r[cols, :] = y.astype(BF16).T
            return 0

        lax.fori_loop(0, len(chunks), one, 0)

    def shared_chunks(chunks):
        def one(j, _):
            cols = pl.ds(al(HID * pick(j, chunks), 128), HID)
            at = al(128 * pick(j, chunks), 128)
            for r in range(16):
                for c in range(5):
                    turn_in[pl.ds(8 * (5 * r + c), 8), :] = packed[
                        1, pl.ds(al(at + 8 * r, 8), 8), pl.ds(128 * c, 128)
                    ]
            turned[...] = turn_in[...].T

            def strip(q, _):
                w = turned[pl.ds(al(q * 16, 16), 16), :]
                for k in range(5):
                    value = scaled(w, 8 + 4 * k, sdn_scales[pl.ds(k, 1), cols])
                    wchunk[pl.ds(al(k * 128 + q * 16, 16), 16), :] = value
                return 0

            lax.fori_loop(0, 8, strip, 0, unroll=2)
            y = jnp.dot(hid_s[...], wchunk[...], preferred_element_type=F32)
            part_s[cols, :] = y.astype(BF16).T
            return 0

        lax.fori_loop(0, len(chunks), one, 0)

    local_tok.wait()
    local_ids.wait()
    expert_row = ids[...]
    onehot = (lax.broadcasted_iota(I32, (16, TOK), 0) == expert_row).astype(F32)
    upto = (
        lax.broadcasted_iota(I32, (TOK, TOK), 0) <= lax.broadcasted_iota(I32, (TOK, TOK), 1)
    ).astype(BF16)
    counted = jnp.dot(onehot.astype(BF16), upto, preferred_element_type=F32)
    rank = jnp.sum(counted * onehot, axis=0, keepdims=True) - 1.0
    slot = expert_row.astype(F32) * 16.0 + rank
    chosen = lax.broadcasted_iota(I32, (SLOTS, TOK), 0).astype(F32) == slot
    select[...] = chosen.astype(F32).astype(BF16)
    disp[...] = lax.dot_general(
        select[...], tk_t[own_rows, :], (((1,), (1,)), ((), ())), preferred_element_type=F32
    ).astype(BF16)
    local_sgu.wait()
    local_sdn.wait()
    local_gs.wait()
    pack_own()

    def a2a(src, dst, k):
        def one(i, _):
            to = lax.rem(exp + i, 16)
            copy(
                src.at[pl.ds(al(16 * to, 16), 16), :],
                dst.at[pl.ds(al(16 * exp, 16), 16), :],
                asend.at[k],
                arecv.at[k],
                {"expert": to},
            ).start()
            return 0

        lax.fori_loop(1, 16, one, 0)
        mine = pl.ds(al(16 * exp, 16), 16)
        dst[mine, :] = src[mine, :]

    def a2a_wait(dst, k):
        ref = dst.at[pl.ds(0, 240), :]
        copy(ref, ref, asend.at[k], arecv.at[k], {"seq": other}).wait_recv()

    def a2a_end(src, k):
        ref = src.at[pl.ds(0, 240), :]
        copy(ref, ref, asend.at[k], arecv.at[k], {"seq": other}).wait_send()

    acc_r[...] = jnp.zeros(acc_r.shape, F32)
    acc_s[...] = jnp.zeros(acc_s.shape, F32)
    unpack_routed(0)
    unpack_routed(1)
    pl.semaphore_wait(barrier, 18)

    first = BLK * lax.rem(z + 4, NZ) // HID

    def chunks_for(offsets, chunks, total):
        qs = [lax.rem(first + q, 5) for q in offsets]
        chunks([5 * other + q for q in qs])
        for q in qs:
            cp = total.sibling_copy(HID * q, HID, q)
            cp.start()
            sent.append(cp)
        chunks([5 * core + q for q in qs])

    def chunks_wait(offsets, total):
        for q in offsets:
            at = lax.rem(first + q, 5)
            total.sibling_wait(HID * at, HID, at)

    def hidden_pair(c, r):
        if c is other:
            slots.sibling_wait(r)
            slots.sibling_wait(-r)
        routed_blocks([block_of(c, r), block_of(c, -r)])

    a2a(disp, disp_in, 0)
    toks.start_whole()
    low.r0()
    high.r0()
    unpack_routed(2)
    unpack_routed(3)
    unpack_routed(4)
    toks.step_whole(1)
    unpack_routed(5)
    unpack_routed(6)
    a2a_wait(disp_in, 0)
    xs_t[own_rows, :] = disp_in[...].T
    slots.start(True)
    unpack_routed(7)
    toks.step_whole(2)
    unpack_routed(8)
    slots.start(False)
    unpack_routed(9)
    local_ss.wait()
    local_sds.wait()
    toks.step_whole(3)
    low.r1()
    high.r1()
    slots.step(1, True)
    slots.sibling_wait(0)
    routed_blocks([block_of(core, 0), block_of(other, 0)])
    toks.step_whole(4)
    slots.step(1, False)
    hidden_pair(core, 1)
    for dz in (0, 1, -1, 2, -2, 3, -3, 4):
        toks.sibling_wait(dz)
    shared_shards(low.arrived(0), 0)
    slots.step(2, True)
    hidden_pair(other, 1)
    shared_shards(low.arrived(1)[0:1], 1)
    slots.step(2, False)
    hidden_pair(core, 2)
    shared_shards(low.arrived(1)[1:3], 2)
    slots.step(3, True)
    hidden_pair(other, 2)
    shared_shards(low.arrived(1)[3:4], 4)
    slots.step(3, False)
    hidden_pair(core, 3)
    low.r2()
    high.r2()
    slots.step(4, True)
    hidden_pair(other, 3)
    slots.sibling_wait(4)
    routed_blocks([block_of(core, 4), block_of(other, 4)])
    activate(acc_r, hid_r)
    local_ds.wait()
    local_dn.wait()
    chunks_for((0, 1), routed_chunks, sum_r)
    chunks_wait((0, 1), sum_r)
    sum_r.long_step(0)
    shared_dot(5)
    chunks_for((4, 2), routed_chunks, sum_r)
    chunks_wait((4, 2), sum_r)
    sum_r.short_step(1)
    sum_r.long_step(1)
    low.r3()
    high.r3()
    chunks_for((3,), routed_chunks, sum_r)
    chunks_wait((3,), sum_r)
    shared_shards(low.arrived(2), 0)
    sum_r.short_step(2)
    low.r4()
    high.r4()
    sum_r.long_step(2)
    shared_dot(6)
    shared_shards(low.arrived(3) + low.arrived(4), 0)
    shared_dot(5)
    activate(acc_s, hid_s)
    sum_r.short_step(3)
    sum_r.long_step(3)
    chunks_for((0, 1), shared_chunks, sum_s)
    chunks_wait((0, 1), sum_s)
    sum_s.long_step(0)
    chunks_for((4, 2), shared_chunks, sum_s)
    chunks_wait((4, 2), sum_s)
    sum_s.short_step(1)
    sum_s.long_step(1)
    back[...] = sum_r.end().astype(BF16).T
    a2a(back, back_in, 1)
    chunks_for((3,), shared_chunks, sum_s)
    chunks_wait((3,), sum_s)
    sum_s.short_step(2)
    sum_s.long_step(2)
    drain(60)
    sum_s.short_step(3)
    sum_s.long_step(3)
    drain(12)
    a2a_end(disp, 0)
    a2a_end(back, 1)
    a2a_wait(back_in, 1)
    local_gate.wait()
    routed = lax.dot_general(
        back_in[...], select[...], (((0,), (0,)), ((), ())), preferred_element_type=F32
    )
    out[...] = (sum_s.end() + gate_w[...] * routed).astype(BF16)

    drain(0)


def shards(
    tokens,
    expert_ids,
    gate_weights,
    gate_up_codes,
    gate_up_scales,
    down_codes,
    down_scales,
    shared_gate_up_codes,
    shared_gate_up_scales,
    shared_down_codes,
    shared_down_scales,
):
    hbm = pl.BlockSpec(memory_space=pl.ANY)
    V = pltpu.VMEM
    S = pltpu.SemaphoreType.DMA
    return pl.pallas_call(
        kernel,
        out_shape=jax.ShapeDtypeStruct((BLK, TOK), BF16),
        in_specs=[hbm] * 11,
        out_specs=pl.BlockSpec(memory_space=pltpu.VMEM),
        scratch_shapes=[
            V((1, TOK), I32),
            V((1, TOK), F32),
            V((50, 2, HID), F32),
            V((5, 1, D), F32),
            V((50, 2, HID), F32),
            V((5, D), F32),
            V((2, 1280, HID), F32),
            V((128, D), F32),
            V((2, 80, HID), F32),
            V((BLK, 128), F32),
            V((2, 1280, HID), I32),
            V((HID, 128), I32),
            V((D, 2 * HID), BF16),
            V((6 * BLK, 2 * HID), BF16),
            V((HID, HID), BF16),
            V((128, HID), I32),
            V((D, SLOTS), BF16),
            V((D, TOK), BF16),
            V((6 * BLK, TOK), BF16),
            V((SLOTS, 2 * HID), F32),
            V((TOK, 2 * HID), F32),
            V((SLOTS, HID), BF16),
            V((TOK, HID), BF16),
            V((D, SLOTS), BF16),
            V((D, TOK), BF16),
            V((3200, SLOTS), BF16),
            V((3200, TOK), BF16),
            V((4, BLK, SLOTS), BF16),
            V((4, BLK, SLOTS), BF16),
            V((4, BLK, TOK), BF16),
            V((4, BLK, TOK), BF16),
            V((SLOTS, TOK), BF16),
            V((SLOTS, BLK), BF16),
            V((SLOTS, BLK), BF16),
            V((SLOTS, BLK), BF16),
            V((SLOTS, BLK), BF16),
            S((40,)),
            S((40,)),
            S((64,)),
            S((64,)),
            S((2,)),
            S((2,)),
            S((48,)),
            S((48,)),
            S((20,)),
        ],
        compiler_params=pltpu.CompilerParams(
            collective_id=0, has_side_effects=True, vmem_limit_bytes=64 * 1024 * 1024 - 65536
        ),
    )(
        tokens.T,
        expert_ids.reshape(1, TOK),
        gate_weights.reshape(1, TOK),
        gate_up_codes[0],
        jnp.transpose(gate_up_scales[0], (1, 0, 2)),
        down_codes[0],
        jnp.transpose(down_scales, (1, 0, 2)),
        shared_gate_up_codes,
        jnp.transpose(shared_gate_up_scales, (1, 0, 2)),
        shared_down_codes.T,
        shared_down_scales,
    ).T


def solution(mesh):
    placed = (
        P("expert", ("seq", "tensor")),
        P("expert"),
        P("expert"),
        P("expert", None, None, ("seq", "tensor")),
        P("expert", None, None, ("seq", "tensor")),
        P("expert", ("seq", "tensor"), None),
        P("expert", ("seq", "tensor"), None),
        P(None, "expert", ("seq", "tensor")),
        P(None, None, ("seq", "tensor")),
        P(("seq", "tensor"), "expert"),
        P(("seq", "tensor"), None),
    )
    return jax.shard_map(
        shards,
        mesh=mesh,
        in_specs=placed,
        out_specs=P("expert", ("seq", "tensor")),
        check_vma=False,
    )
```
